32 devices in a mesh: dp: 8 (over z, x), row: 2 (over y), col: 2 (over core).
Axes of the slice: x: 2, y: 2, z: 4, core: 2. Of those that a mesh axis runs over, the one named last changes fastest.
Arguments:
- tokens: bfloat16 [25216, 768], P(('dp', 'row', 'col')), may hold values from -6 to 6
- out_grad: bfloat16 [25216, 768], P(('dp', 'row', 'col')), may hold values from -6 to 6
- routes: int32 [25216, 2], P(('dp', 'row', 'col')), may hold values from 0 to 15, all different within a row
- slot_order: int32 [32, 1576], P(('dp', 'row', 'col')), may hold values from 0 to 1575, each once within a row
- norm_params: float32 [768, 4], P(('dp', 'row', 'col')), may hold values from -0.5 to 5
- qkv_weight: float32 [768, 3, 768], P(('dp', 'row', 'col')), may hold values from -0.21875 to 0.21875
- proj_weight: float32 [768, 768], P(('dp', 'row', 'col')), may hold values from -0.875 to 0.875
- router_weight: float32 [768, 16], P(('dp', 'row', 'col')), may hold values from -0.15625 to 0.15625
- inner_weight: float32 [16, 768, 3072], P(('dp', 'col'), None, 'row'), may hold values from -1 to 1
- outer_weight: float32 [16, 3072, 768], P(('dp', 'col'), 'row'), may hold values from -0.15625 to 0.15625
- norm_moment: float32 [768, 4], P(('dp', 'row', 'col')), may hold values from -1 to 1
- norm_second: float32 [768, 4], P(('dp', 'row', 'col')), may hold values from 0 to 1, as said below
- qkv_moment: float32 [768, 3, 768], P(('dp', 'row', 'col')), may hold values from -1 to 1
- qkv_second: float32 [768, 3, 768], P(('dp', 'row', 'col')), may hold values from 0 to 1, as said below
- proj_moment: float32 [768, 768], P(('dp', 'row', 'col')), may hold values from -1 to 1
- proj_second: float32 [768, 768], P(('dp', 'row', 'col')), may hold values from 0 to 1, as said below
- router_moment: float32 [768, 16], P(('dp', 'row', 'col')), may hold values from -1 to 1
- router_second: float32 [768, 16], P(('dp', 'row', 'col')), may hold values from 0 to 1, as said below
- inner_moment: float32 [16, 768, 3072], P(('dp', 'col'), None, 'row'), may hold values from -1 to 1
- inner_second: float32 [16, 768, 3072], P(('dp', 'col'), None, 'row'), may hold values from 0 to 1, as said below
- outer_moment: float32 [16, 3072, 768], P(('dp', 'col'), 'row'), may hold values from -1 to 1
- outer_second: float32 [16, 3072, 768], P(('dp', 'col'), 'row'), may hold values from 0 to 1, as said below
Outputs:
- block_out: bfloat16 [25216, 768], P(('dp', 'row', 'col'))
- tokens_grad: float32 [25216, 768], P(('dp', 'row', 'col'))
- grad_norm: float32 [], replicated
- norm_moment_new: float32 [768, 4], P(('dp', 'row', 'col'))
- norm_second_new: float32 [768, 4], P(('dp', 'row', 'col'))
- norm_params_new: float32 [768, 4], P(('dp', 'row', 'col'))
- qkv_moment_new: float32 [768, 3, 768], P(('dp', 'row', 'col'))
- qkv_second_new: float32 [768, 3, 768], P(('dp', 'row', 'col'))
- qkv_weight_new: float32 [768, 3, 768], P(('dp', 'row', 'col'))
- proj_moment_new: float32 [768, 768], P(('dp', 'row', 'col'))
- proj_second_new: float32 [768, 768], P(('dp', 'row', 'col'))
- proj_weight_new: float32 [768, 768], P(('dp', 'row', 'col'))
- router_moment_new: float32 [768, 16], P(('dp', 'row', 'col'))
- router_second_new: float32 [768, 16], P(('dp', 'row', 'col'))
- router_weight_new: float32 [768, 16], P(('dp', 'row', 'col'))
- inner_moment_new: float32 [16, 768, 3072], P(('dp', 'col'), None, 'row')
- inner_second_new: float32 [16, 768, 3072], P(('dp', 'col'), None, 'row')
- inner_weight_new: float32 [16, 768, 3072], P(('dp', 'col'), None, 'row')
- outer_moment_new: float32 [16, 3072, 768], P(('dp', 'col'), 'row')
- outer_second_new: float32 [16, 3072, 768], P(('dp', 'col'), 'row')
- outer_weight_new: float32 [16, 3072, 768], P(('dp', 'col'), 'row')
The draws below stay inside these ranges and needn't reach their ends.
Inputs may be any that keep to these rules, and one draw needn't show every extreme that they name: `routes`: each row names 2 different experts. `slot_order`: each row is an ordering of the 1576 pairs of one device. `norm_second`: positive. `qkv_second`: positive. `proj_second`: positive. `router_second`: positive. `inner_second`: positive. `outer_second`: positive.
All inputs are finite; a program needn't handle non-finite values.
Results may differ from the reference program's by a relative error of at most 0.015.
The reference program's roundings to bfloat16 on the way count: a program that leaves them out, or rounds other values in their place, can miss the bound.
Values may be sent and summed in bfloat16 or wider, within the bound.
No kernel may reach another device: no remote copies, remote signals or barrier semaphores. Data moves between devices by JAX's collectives and lax.ppermute only.
A program may use at most 256 MiB of HBM per device.

```python
import math
from functools import partial
import jax
import jax.numpy as jnp
from jax import lax

D = 768
HEADS = 12
HEAD = 64
FF = 3072
SEQ = 197
TOPK = 2
STEP = 10
TOK_DEV = 788
PAIRS = 1576
TOKENS = 25216
EXPERTS = 16
CAP = 124
N_DP = 8
N_ROW = 2
N_COL = 2


def clipped_square(coefficient):
    return coefficient / (0.19 * D * D + 72.0 * D + 0.17 * D * FF + 4.0 * D)


def first_draw(key, out_shape, coefficient):
    noise_vals = jnp.clip(jax.random.normal(key, out_shape, jnp.float32), -4.0, 4.0)
    return noise_vals * (0.111 * math.sqrt(clipped_square(coefficient)))


def second_draw(key, out_shape, coefficient):
    spread = jax.random.uniform(key, out_shape, jnp.float32, math.log(0.0005), math.log(0.008))
    return jnp.exp(spread) * clipped_square(coefficient)


def draw_norm_params(key, part):
    key = jax.random.fold_in(key, 1)
    gain_key, bias_key = jax.random.split(key)
    ramp = jnp.arange(D, dtype=jnp.float32)[:, None] / D
    rough = jax.random.uniform(gain_key, (D, 2), jnp.float32, 0.7, 1.3)
    gain_vals = 0.6 * jnp.power(3.0, ramp) * rough
    bias_vals = jnp.clip(0.1 * jax.random.normal(bias_key, (D, 2), jnp.float32), -0.3, 0.3)
    return jnp.stack([gain_vals[:, 0], bias_vals[:, 0], gain_vals[:, 1], bias_vals[:, 1]], axis=1)


def draw_inner_weight(key, part):
    key = jax.random.fold_in(key, 2)
    expert_ramp = jnp.arange(EXPERTS, dtype=jnp.float32)[:, None, None] / EXPERTS
    unit_ramp = jnp.arange(FF, dtype=jnp.float32)[None, None, :] / FF
    base_val = 3.0
    noise_vals = jnp.clip(jax.random.normal(key, (EXPERTS, D, FF), jnp.float32), -4.0, 4.0)
    return noise_vals * jnp.power(base_val, 0.5 * expert_ramp + 0.5 * unit_ramp) / math.sqrt(D)


def draw_norm_moment(key, part):
    key = jax.random.fold_in(key, 3)
    return first_draw(key, (D, 4), 1.0)


def draw_norm_second(key, part):
    key = jax.random.fold_in(key, 4)
    return second_draw(key, (D, 4), 1.0)


def draw_qkv_moment(key, part):
    key = jax.random.fold_in(key, 5)
    return first_draw(key, (D, 3, D), 0.05)


def draw_qkv_second(key, part):
    key = jax.random.fold_in(key, 6)
    return second_draw(key, (D, 3, D), 0.05)


def draw_proj_moment(key, part):
    key = jax.random.fold_in(key, 7)
    return first_draw(key, (D, D), 0.04)


def draw_proj_second(key, part):
    key = jax.random.fold_in(key, 8)
    return second_draw(key, (D, D), 0.04)


def draw_router_moment(key, part):
    key = jax.random.fold_in(key, 9)
    return first_draw(key, (D, EXPERTS), 72.0 / EXPERTS)


def draw_router_second(key, part):
    key = jax.random.fold_in(key, 10)
    return second_draw(key, (D, EXPERTS), 72.0 / EXPERTS)


def draw_inner_moment(key, part):
    key = jax.random.fold_in(key, 11)
    return first_draw(key, (EXPERTS, D, FF), 0.0315 / EXPERTS)


def draw_inner_second(key, part):
    key = jax.random.fold_in(key, 12)
    return second_draw(key, (EXPERTS, D, FF), 0.0315 / EXPERTS)


def draw_outer_moment(key, part):
    key = jax.random.fold_in(key, 13)
    return first_draw(key, (EXPERTS, FF, D), 0.14 / EXPERTS)


def draw_outer_second(key, part):
    key = jax.random.fold_in(key, 14)
    return second_draw(key, (EXPERTS, FF, D), 0.14 / EXPERTS)


def shard_levels(key, shape, cuts, least, high):
    loudness = 1.0
    for axis_at, parts in cuts:
        steps = jax.random.uniform(jax.random.fold_in(jax.random.fold_in(key, 6), axis_at), (parts,), jnp.float32, least / len(cuts), high / len(cuts))
        loudness = loudness * jnp.repeat(jnp.exp(steps), shape[axis_at] // parts).reshape((-1,) + (1,) * (len(shape) - 1 - axis_at))
    return loudness


def choose_distinct(own_key, rows, number_of, top, lift):
    order = jax.random.permutation(jax.random.fold_in(own_key, 1), number_of)
    favour = order
    for power in range(3):
        favour = favour * favour // number_of
    favour = favour * lift // number_of
    chance = jax.random.randint(jax.random.fold_in(own_key, 2), (rows, number_of), 0, 4096) + favour
    sure = jax.random.permutation(jax.random.fold_in(own_key, 3), rows)[jnp.arange(number_of) % rows]
    chance = jnp.where(jnp.arange(rows)[:, None] == sure[None, :], 1 << 14, chance)
    score = chance * number_of + jnp.arange(number_of)
    return lax.top_k(score.astype(jnp.int32), top)[1].astype(jnp.int32)


def bell_draw(stream_key, dims, scale, limit, shards=(), kind=jnp.bfloat16):
    level = shard_levels(stream_key, dims, shards, -0.22, 0.18) if shards else 1.0
    drawn = jax.random.normal(stream_key, dims, jnp.float32) * scale * level
    return jnp.minimum(jnp.maximum(drawn, -limit), limit).astype(kind)


def setup_inputs(seed: int = 0) -> dict:
    key_list = jax.random.split(jax.random.key(seed), 23)
    return {
        "tokens": bell_draw(key_list[0], (TOKENS, D), 1.0, 6.0, ((0, 32),)),
        "out_grad": bell_draw(key_list[1], (TOKENS, D), 1.0, 6.0, ((0, 32),)),
        "routes": choose_distinct(key_list[2], TOKENS, EXPERTS, TOPK, 1024),
        "slot_order": jax.vmap(lambda own: jax.random.permutation(own, PAIRS))(jax.random.split(key_list[3], (N_DP * N_ROW * N_COL))).reshape((N_DP * N_ROW * N_COL, PAIRS)).astype(jnp.int32),
        "norm_params": draw_norm_params(jax.random.fold_in(key_list[22], 71), 0),
        "qkv_weight": bell_draw(key_list[5], (D, 3, D), D ** -0.5, 0.21875, ((0, 32),), jnp.float32),
        "proj_weight": bell_draw(key_list[6], (D, D), (D // 16) ** -0.5, 0.875, ((0, 32),), jnp.float32),
        "router_weight": bell_draw(key_list[7], (D, EXPERTS), (2 * D) ** -0.5, 0.15625, ((0, 32),), jnp.float32),
        "inner_weight": draw_inner_weight(jax.random.fold_in(key_list[22], 71), 0),
        "outer_weight": bell_draw(key_list[9], (EXPERTS, FF, D), (FF // 2) ** -0.5, 0.15625, ((0, 16), (1, 2)), jnp.float32),
        "norm_moment": draw_norm_moment(jax.random.fold_in(key_list[22], 71), 0),
        "norm_second": draw_norm_second(jax.random.fold_in(key_list[22], 71), 0),
        "qkv_moment": draw_qkv_moment(jax.random.fold_in(key_list[22], 71), 0),
        "qkv_second": draw_qkv_second(jax.random.fold_in(key_list[22], 71), 0),
        "proj_moment": draw_proj_moment(jax.random.fold_in(key_list[22], 71), 0),
        "proj_second": draw_proj_second(jax.random.fold_in(key_list[22], 71), 0),
        "router_moment": draw_router_moment(jax.random.fold_in(key_list[22], 71), 0),
        "router_second": draw_router_second(jax.random.fold_in(key_list[22], 71), 0),
        "inner_moment": draw_inner_moment(jax.random.fold_in(key_list[22], 71), 0),
        "inner_second": draw_inner_second(jax.random.fold_in(key_list[22], 71), 0),
        "outer_moment": draw_outer_moment(jax.random.fold_in(key_list[22], 71), 0),
        "outer_second": draw_outer_second(jax.random.fold_in(key_list[22], 71), 0),
    }


NORM_EPS = 1e-06
CLIP_NORM = 1.0
BETA_ONE = 0.9
BETA_TWO = 0.999
ADAM_EPS = 1e-08
RATE_MATRIX = 0.08
RATE_NORM = 0.4
DECAY_MATRIX = 0.1
HIGH = lax.Precision.HIGHEST

@jax.custom_vjp
def low(v):
    return lax.optimization_barrier(v.astype(jnp.bfloat16)).astype(jnp.float32)

@jax.custom_vjp
def low_back(v):
    return v

def low_keep(v):
    return (low(v), None)

def low_pass(kept, grad):
    return (grad,)

def back_keep(v):
    return (v, None)

def back_low(kept, grad):
    return (low(grad),)
low.defvjp(low_keep, low_pass)
low_back.defvjp(back_keep, back_low)

def layer_norm(tok_rows, gain_vec, bias_vec):
    mean_val = lax.optimization_barrier(jnp.mean(tok_rows, axis=-1, keepdims=True))
    centred = tok_rows - mean_val
    spread_val = lax.optimization_barrier(jnp.mean(centred * centred, axis=-1, keepdims=True))
    return centred * lax.rsqrt(spread_val + NORM_EPS) * gain_vec + bias_vec

def gelu_exact(values):
    return jax.nn.gelu(values, approximate=False)

def device_slots(route_rows, order_row):
    pair_expert = route_rows.reshape(-1).astype(jnp.int32)
    ranked = pair_expert[order_row]
    hit_table = (ranked[:, None] == jnp.arange(EXPERTS, dtype=jnp.int32)[None, :]).astype(jnp.int32)
    before = jnp.cumsum(hit_table, axis=0) - hit_table
    ranked_pos = lax.optimization_barrier(jnp.sum(before * hit_table, axis=1)).astype(jnp.int32)
    position = jnp.zeros((PAIRS,), jnp.int32).at[order_row].set(ranked_pos)
    return jnp.where(position < CAP, pair_expert * CAP + position, EXPERTS * CAP).astype(jnp.int32)

def pair_tables(routes, slot_order):
    devices = N_DP * N_ROW * N_COL
    slot_rows = jax.vmap(device_slots)(routes.reshape(devices, TOK_DEV, TOPK), slot_order)
    local_pairs = jnp.arange(PAIRS, dtype=jnp.int32)

    def place_pairs(slot_row):
        return jnp.full((EXPERTS * CAP + 1,), PAIRS, jnp.int32).at[slot_row].set(local_pairs)[:-1]
    slot_pair = jax.vmap(place_pairs)(slot_rows)
    offsets = (jnp.arange(devices, dtype=jnp.int32) * PAIRS)[:, None]
    global_pair = jnp.where(slot_pair < PAIRS, slot_pair + offsets, devices * PAIRS).astype(jnp.int32)
    return global_pair.reshape(devices, EXPERTS, CAP).transpose(1, 0, 2).reshape(EXPERTS, devices * CAP)

def attend_block(tok_rows, norm_low, qkv_low, proj_low):
    normed = low(layer_norm(tok_rows, norm_low[:, 0], norm_low[:, 1]))
    projected = jnp.einsum('td,dsf->tsf', normed, qkv_low, precision=HIGH)
    projected = low_back(low(projected)).reshape(-1, SEQ, 3, HEADS, HEAD)
    queries = projected[:, :, 0]
    key_rows = projected[:, :, 1]
    value_rows = projected[:, :, 2]
    scores = low_back(jnp.einsum('ishd,ijhd->ihsj', queries, key_rows, precision=HIGH) * HEAD ** (-0.5))
    weights = low(jax.nn.softmax(scores, axis=-1))
    mixed = jnp.einsum('ihsj,ijhd->ishd', weights, value_rows, precision=HIGH)
    mixed = low_back(low(mixed)).reshape(-1, D)
    return tok_rows + low_back(jnp.einsum('tf,of->to', mixed, proj_low, precision=HIGH))

def expert_term(inner_one, outer_one, pair_index, gate_rows, normed_pad):
    gathered = low_back(normed_pad[pair_index // TOPK])
    inner_act = low_back(jnp.dot(gathered, low(inner_one), precision=HIGH))
    hidden = low(gelu_exact(inner_act))
    result = low_back(low(jnp.dot(hidden, low(outer_one), precision=HIGH)))
    return gate_rows[:, None] * result

def forward(tok_rows, norm_params, qkv_weight, proj_weight, router_weight, inner_weight, outer_weight, routes, global_pair):
    norm_low = low(norm_params)
    block_fn = jax.checkpoint(partial(attend_block, norm_low=norm_low, qkv_low=low(qkv_weight), proj_low=low(proj_weight)))
    blocks = tok_rows.reshape(-1, 8 * TOK_DEV, D)
    after_attn = lax.map(block_fn, blocks).reshape(TOKENS, D)
    normed = low(layer_norm(after_attn, norm_low[:, 2], norm_low[:, 3]))
    logits = low_back(jnp.dot(normed, low(router_weight), precision=HIGH))
    gate_vals = jax.nn.softmax(jnp.take_along_axis(logits, routes, axis=1), axis=-1)
    gate_pad = jnp.concatenate([gate_vals.reshape(-1), jnp.zeros((1,), jnp.float32)])
    normed_pad = jnp.concatenate([normed, jnp.zeros((1, D), jnp.float32)])
    expert_fn = jax.checkpoint(expert_term)

    def add_expert(summed, pieces):
        inner_one, outer_one, pair_index = pieces
        contrib = expert_fn(inner_one, outer_one, pair_index, gate_pad[pair_index], normed_pad)
        return (summed.at[pair_index // TOPK].add(contrib), None)
    summed, _unused = lax.scan(add_expert, jnp.zeros((TOKENS + 1, D), jnp.float32), (inner_weight, outer_weight, global_pair))
    return after_attn + summed[:TOKENS]

def adam_update(weight, gradient, moment_one, moment_two, clip_scale, rate_val, decay_val):
    clipped = gradient * clip_scale
    first_new = BETA_ONE * moment_one + (1.0 - BETA_ONE) * clipped
    second_new = BETA_TWO * moment_two + (1.0 - BETA_TWO) * clipped * clipped
    first_hat = first_new / (1.0 - BETA_ONE ** STEP)
    second_hat = second_new / (1.0 - BETA_TWO ** STEP)
    return (first_new, second_new, weight - rate_val * (first_hat / (jnp.sqrt(second_hat) + ADAM_EPS) + decay_val * weight))

def reference(tokens, out_grad, routes, slot_order, norm_params, qkv_weight, proj_weight, router_weight, inner_weight, outer_weight, norm_moment, norm_second, qkv_moment, qkv_second, proj_moment, proj_second, router_moment, router_second, inner_moment, inner_second, outer_moment, outer_second):
    global_pair = pair_tables(routes, slot_order)

    def layer_fn(tok_rows, norm_vals, qkv_vals, proj_vals, router_vals, inner_vals, outer_vals):
        return forward(tok_rows, norm_vals, qkv_vals, proj_vals, router_vals, inner_vals, outer_vals, routes, global_pair)
    layer_out, pullback = jax.vjp(layer_fn, tokens.astype(jnp.float32), norm_params, qkv_weight, proj_weight, router_weight, inner_weight, outer_weight)
    gradients = pullback(out_grad.astype(jnp.float32))
    tokens_grad, norm_grad, qkv_grad, proj_grad, router_grad, inner_grad, outer_grad = gradients
    square_sum = jnp.sum(norm_grad * norm_grad) + jnp.sum(qkv_grad * qkv_grad) + jnp.sum(proj_grad * proj_grad) + jnp.sum(router_grad * router_grad) + jnp.sum(inner_grad * inner_grad) + jnp.sum(outer_grad * outer_grad)
    grad_norm = jnp.sqrt(square_sum)
    clip_scale = jnp.minimum(1.0, CLIP_NORM / (grad_norm + 1e-06))
    norm_m, norm_s, norm_w = adam_update(norm_params, norm_grad, norm_moment, norm_second, clip_scale, RATE_NORM, 0.0)
    qkv_m, qkv_s, qkv_w = adam_update(qkv_weight, qkv_grad, qkv_moment, qkv_second, clip_scale, RATE_MATRIX, DECAY_MATRIX)
    proj_m, proj_s, proj_w = adam_update(proj_weight, proj_grad, proj_moment, proj_second, clip_scale, RATE_MATRIX, DECAY_MATRIX)
    router_m, router_s, router_w = adam_update(router_weight, router_grad, router_moment, router_second, clip_scale, RATE_MATRIX, DECAY_MATRIX)
    inner_m, inner_s, inner_w = adam_update(inner_weight, inner_grad, inner_moment, inner_second, clip_scale, RATE_MATRIX, DECAY_MATRIX)
    outer_m, outer_s, outer_w = adam_update(outer_weight, outer_grad, outer_moment, outer_second, clip_scale, RATE_MATRIX, DECAY_MATRIX)
    return (layer_out.astype(jnp.bfloat16), tokens_grad, grad_norm, norm_m, norm_s, norm_w, qkv_m, qkv_s, qkv_w, proj_m, proj_s, proj_w, router_m, router_s, router_w, inner_m, inner_s, inner_w, outer_m, outer_s, outer_w)
```

```python
import functools

import jax
import jax.numpy as jnp
from jax import lax
from jax.experimental import pallas as pl
from jax.experimental.pallas import tpu as pltpu
from jax.sharding import PartitionSpec as P

HEADS = 12
HEAD = 64
SEQ = 197
STEP = 10

NORM_EPS = 1e-06
CLIP_NORM = 1.0
BETA_ONE = 0.9
BETA_TWO = 0.999
ADAM_EPS = 1e-08
RATE_MATRIX = 0.08
RATE_NORM = 0.4
DECAY_MATRIX = 0.1

LANES = 128
MIB = 1024 * 1024
SMALL_COST = pl.CostEstimate(flops=1024, bytes_accessed=1024, transcendentals=0)
ALL = ("dp", "row", "col")
GROUP = ("dp", "col")
BF = jnp.bfloat16
F32 = jnp.float32

ERFC_P = 0.39
LOG2_E = 1.4426950408889634
ERFC_C = (
    0.23532534336933997,
    0.09138763496502661,
    0.649561341403834,
    -0.6354026835533981,
    0.8866658487971544,
    -0.2275374866853928,
)


def round_up(value, unit):
    return -(-value // unit) * unit


def dot_nn(a, b):
    return lax.dot_general(a, b, (((1,), (0,)), ((), ())), preferred_element_type=F32)


def dot_nt(a, b):
    return lax.dot_general(a, b, (((1,), (1,)), ((), ())), preferred_element_type=F32)


def dot_tn(a, b):
    return lax.dot_general(a, b, (((0,), (0,)), ((), ())), preferred_element_type=F32)


def iota(shape, dim):
    return lax.broadcasted_iota(jnp.int32, shape, dim)


def ones_where(cond):
    return jnp.where(cond, 1.0, 0.0)


def split_three(value):
    high = value.astype(BF)
    rest = value - high.astype(F32)
    middle = rest.astype(BF)
    low = (rest - middle.astype(F32)).astype(BF)
    return high, middle, low


def kernel_params(mebibytes):
    return pltpu.CompilerParams(vmem_limit_bytes=mebibytes * MIB)


def norm_parts(rows):
    mean_val = jnp.mean(rows, axis=-1, keepdims=True)
    centred = rows - mean_val
    spread_val = jnp.mean(centred * centred, axis=-1, keepdims=True)
    inv = lax.rsqrt(spread_val + NORM_EPS)
    return centred * inv, inv


def norm_back(upstream, gain, normal, inv):
    scaled = upstream * gain
    return inv * (
        scaled
        - jnp.mean(scaled, axis=-1, keepdims=True)
        - normal * jnp.mean(scaled * normal, axis=-1, keepdims=True)
    )


class Sizes:
    def __init__(self, tok_count, width, choose, experts):
        self.tok = tok_count
        self.width = width
        self.choose = choose
        self.experts = experts
        self.pairs = tok_count * choose
        self.cap = max(2, (5 * self.pairs + 4 * experts - 1) // (4 * experts))
        half = 16
        while 2 * (half - 1) < self.cap:
            half *= 2
        self.half = half
        self.chunk = experts * half
        self.images = tok_count // SEQ
        self.seq_pad = round_up(SEQ, 32)
        self.rows = self.images * self.seq_pad
        self.rank = round_up(self.pairs, 256)
        self.packed = round_up(4 * width + experts + 4, LANES)
        self.part_one = 2 * width
        self.part_two = self.packed - self.part_one


def slots_kernel(sz, order_ref, routes_ref, dy_ref, slot_ref, send_ref, hot_ref):
    rows, rank, experts, half, chunk = sz.rows, sz.rank, sz.experts, sz.half, sz.chunk
    order = order_ref[...]
    ranked = jnp.zeros((experts, rank), F32)
    for start in range(0, sz.choose * rows, 256):
        size = min(256, sz.choose * rows - start)
        hit = ones_where(order == iota((size, rank), 0) + start).astype(BF)
        hot_ref[start : start + size, :] = hit
        kind = ones_where(
            routes_ref[0:1, start : start + size] == iota((experts, size), 0)
        ).astype(BF)
        ranked += dot_nn(kind, hit)
    ranked_low = ranked.astype(BF)
    before = jnp.zeros((experts, rank), F32)
    for start in range(0, rank, 256):
        earlier = ones_where(iota((256, rank), 0) + start < iota((256, rank), 1)).astype(BF)
        before += dot_nn(ranked_low[:, start : start + 256], earlier)
    position = jnp.sum(before * ranked, axis=0, keepdims=True)
    named = jnp.sum(ranked * iota((experts, rank), 0).astype(F32), axis=0, keepdims=True)
    real = jnp.sum(ranked, axis=0, keepdims=True)
    kept = real * ones_where(position < sz.cap)
    second = ones_where(position >= half - 1)
    row_in = position + 1.0 - second * (half - 1)
    row_in = jnp.where(kept > 0.5, row_in, 0.0)
    part = iota((16, rank), 0)
    codes = jnp.where(
        part == 0, named, jnp.where(part == 1, row_in, jnp.where(part == 2, second, kept))
    )
    codes = jnp.where(part < 4, codes, 0.0).astype(BF)
    wide = iota((LANES, rows), 0)
    table = jnp.full((LANES, rows), -1.0, F32)
    for k in range(sz.choose):
        route = routes_ref[0:1, k * rows : (k + 1) * rows].astype(F32)
        table = jnp.where(wide == sz.choose + k, route, table)
    for k in range(sz.choose):
        back = dot_nt(codes, hot_ref[k * rows : (k + 1) * rows, :])
        slot = jnp.where(
            back[3:4] > 0.5, back[2:3] * chunk + back[0:1] * half + back[1:2], -1.0
        )
        table = jnp.where(wide == k, slot, table)
    slot_ref[...] = table[0:8].astype(jnp.int32)
    slots = slot_ref[...]
    block = min(256, chunk)
    dy = dy_ref[...]
    for c in range(2):
        for start in range(0, chunk, block):
            ids = iota((block, rows), 0) + (c * chunk + start)
            pick = ids == slots[0:1]
            for k in range(1, sz.choose):
                pick = pick | (ids == slots[k : k + 1])
            moved = dot_nn(ones_where(pick).astype(BF), dy).astype(BF)
            send_ref[start // half : (start + block) // half, c * half : (c + 1) * half] = (
                moved.reshape(block // half, half, sz.width)
            )


def call_slots(sz, order, routes_row, dy):
    return pl.pallas_call(
        functools.partial(slots_kernel, sz),
        out_shape=(
            jax.ShapeDtypeStruct((8, sz.rows), jnp.int32),
            jax.ShapeDtypeStruct((sz.experts, 2 * sz.half, sz.width), BF),
        ),
        scratch_shapes=[pltpu.VMEM((sz.choose * sz.rows, sz.rank), BF)],
        compiler_params=kernel_params(56),
        cost_estimate=SMALL_COST,
        name="slots",
    )(order, routes_row, dy)


def attend_kernel(
    sz,
    tok_ref,
    w_one_ref,
    w_two_ref,
    routes_ref,
    slot_ref,
    qkv_ref,
    lse_ref,
    mixed_ref,
    after_ref,
    normed_ref,
    gate_ref,
    gate_col_ref,
    send_one_ref,
    send_two_ref,
    normed_all,
    tail_t,
):
    width, seq, rows = sz.width, sz.seq_pad, sz.rows
    step = pl.program_id(0)

    @pl.when(step == 0)
    def _():
        tail_t[...] = w_two_ref[:, 2 * width :].astype(F32).T

    first = sz.experts
    gain_one, bias_one = tail_t[first : first + 1], tail_t[first + 1 : first + 2]
    gain_two, bias_two = tail_t[first + 2 : first + 3], tail_t[first + 3 : first + 4]
    tok = tok_ref[...].astype(F32)
    normal, _ = norm_parts(tok)
    normed = (normal * gain_one + bias_one).astype(BF)
    qkv_ref[:, : 2 * width] = dot_nn(normed, w_one_ref[...]).astype(BF)
    qkv_ref[:, 2 * width :] = dot_nn(normed, w_two_ref[:, :width]).astype(BF)
    lane = iota((seq, LANES), 1)
    key_ok = iota((seq, seq), 0) < SEQ
    pair_lane = iota((1, LANES), 1) // HEAD
    for j in range(HEADS // 2):
        at = j * LANES
        q = qkv_ref[:, at : at + LANES]
        key = qkv_ref[:, width + at : width + at + LANES]
        val = qkv_ref[:, 2 * width + at : 2 * width + at + LANES]
        outs = []
        for a in range(2):
            own = jnp.where(pair_lane == a, HEAD**-0.5, 0.0).astype(BF)
            scores = jnp.where(key_ok, dot_nt(key, q * own), -1e30)
            top = jnp.max(scores, axis=0, keepdims=True)
            raised = jnp.exp(scores - top)
            total = jnp.sum(raised, axis=0, keepdims=True)
            probs = (raised * (1.0 / total)).astype(BF)
            outs.append(dot_tn(probs, val))
            lse_ref[2 * j + a : 2 * j + a + 1, :] = top + jnp.log(total)
        mixed_ref[:, at : at + LANES] = jnp.where(lane < HEAD, outs[0], outs[1]).astype(BF)
    after = tok + dot_nt(mixed_ref[...], w_two_ref[:, width : 2 * width])
    after_ref[...] = after
    normal, _ = norm_parts(after)
    normed_two = (normal * gain_two + bias_two).astype(BF)
    normed_ref[...] = normed_two
    normed_all[pl.ds(step * seq, seq), :] = normed_two

    @pl.when(step == sz.images - 1)
    def _():
        normed_two = normed_all[...]
        logits = dot_nt(tail_t[...].astype(BF), normed_two)
        kinds = iota((LANES, rows), 0)
        chosen = [
            jnp.sum(jnp.where(kinds == routes_ref[k : k + 1], logits, 0.0), axis=0, keepdims=True)
            for k in range(sz.choose)
        ]
        top = functools.reduce(jnp.maximum, chosen)
        raised = [jnp.exp(c - top) for c in chosen]
        total = functools.reduce(jnp.add, raised)
        gates = [r / total for r in raised]
        wide = jnp.zeros((LANES, rows), F32)
        for k in range(sz.choose):
            wide = jnp.where(kinds == k, gates[k], wide)
        gate_ref[...] = wide[0:8]
        gate_col_ref[...] = wide.T
        half, chunk = sz.half, sz.chunk
        part = iota((16, rows), 0)
        coded = []
        for k in range(sz.choose):
            pieces = split_three(gates[k])
            table = jnp.zeros((16, rows), F32)
            for m in range(3):
                table = jnp.where(part == m, pieces[m].astype(F32), table)
            coded.append(table.astype(BF))
        block = min(256, chunk)
        for c, out_ref in enumerate((send_one_ref, send_two_ref)):
            for start in range(0, chunk, block):
                ids = iota((block, rows), 0) + (c * chunk + start)
                picks = [
                    ones_where(ids == slot_ref[k : k + 1]).astype(BF) for k in range(sz.choose)
                ]
                moved = dot_nn(functools.reduce(jnp.add, picks), normed_two)
                meta = functools.reduce(
                    jnp.add, [dot_nt(coded[k], picks[k]) for k in range(sz.choose)]
                )
                for e in range(block // half):
                    base, shift = (e * half) // LANES * LANES, (e * half) % LANES
                    near = meta[0:8, base : base + LANES] if block >= LANES else meta[0:8]
                    if shift:
                        near = pltpu.roll(near, LANES - shift, axis=1)
                    line = jnp.concatenate(
                        [near[0:1], near[1:2], near[2:3], jnp.zeros((1, width - 3 * LANES), F32)],
                        axis=1,
                    )
                    body = moved[e * half : (e + 1) * half]
                    body = jnp.where(iota((half, width), 0) == 0, line, body)
                    at = start + e * half
                    out_ref[at : at + half, :] = body.astype(BF)


def call_attend(sz, tok, packed, routes_row, slots):
    images, seq, width, rows = sz.images, sz.seq_pad, sz.width, sz.rows
    per_image = lambda size: pl.BlockSpec((None, seq, size), lambda i: (i, 0, 0))
    lse_spec = pl.BlockSpec((None, 16, seq), lambda i: (i, 0, 0))
    whole = lambda *shape: pl.BlockSpec(shape, lambda i: (0,) * len(shape))
    return pl.pallas_call(
        functools.partial(attend_kernel, sz),
        grid=(images,),
        in_specs=[
            per_image(width),
            whole(width, sz.part_one),
            whole(width, sz.part_two),
            whole(8, rows),
            whole(8, rows),
        ],
        out_specs=(
            per_image(3 * width),
            lse_spec,
            per_image(width),
            per_image(width),
            per_image(width),
            whole(8, rows),
            whole(rows, LANES),
            whole(sz.chunk, width),
            whole(sz.chunk, width),
        ),
        out_shape=(
            jax.ShapeDtypeStruct((images, seq, 3 * width), BF),
            jax.ShapeDtypeStruct((images, 16, seq), F32),
            jax.ShapeDtypeStruct((images, seq, width), BF),
            jax.ShapeDtypeStruct((images, seq, width), F32),
            jax.ShapeDtypeStruct((images, seq, width), BF),
            jax.ShapeDtypeStruct((8, rows), F32),
            jax.ShapeDtypeStruct((rows, LANES), F32),
            jax.ShapeDtypeStruct((sz.chunk, width), BF),
            jax.ShapeDtypeStruct((sz.chunk, width), BF),
        ),
        scratch_shapes=[pltpu.VMEM((rows, width), BF), pltpu.VMEM((LANES, width), F32)],
        compiler_params=kernel_params(56),
        cost_estimate=SMALL_COST,
        name="attend",
    )(tok, *packed, routes_row, slots)


def own_copies(per_ring, block, in_own, out_own, w_in, w_out):
    copies = []
    for j in range(per_ring):
        cols = slice(j * block, (j + 1) * block)
        copies.append((j, in_own.at[:, cols], w_in.at[j]))
        copies.append((j, out_own.at[cols, :], w_out.at[j]))
    return copies


def far_copies(ring, per_ring, block, first_step, in_far, out_far, w_in, w_out):
    copies = []
    for r in range(ring - 1):
        for j in range(per_ring):
            step, start = first_step + per_ring * r + j, j * block
            at = 0
            for piece in in_far:
                rows = slice(at, at + piece.shape[1])
                copies.append(
                    (step, piece.at[r, :, start : start + block], w_in.at[step, rows, :])
                )
                at += piece.shape[1]
            at = 0
            for piece in out_far:
                first, last = max(at, start), min(at + piece.shape[1], start + block)
                if first < last:
                    copies.append(
                        (
                            step,
                            piece.at[r, first - at : last - at, :],
                            w_out.at[step, first - start : last - start, :],
                        )
                    )
                at += piece.shape[1]
    return copies


def expert_kernel(sz, ring, per_ring, own, far, extra, in_count, out_count, *refs):
    refs = list(refs)
    take = lambda count: [refs.pop(0) for _ in range(count)]
    x_ref, dy_ref = take(2)
    in_own, out_own = take(2) if own else (None, None)
    in_far, out_far = take(in_count if far else 0), take(out_count if far else 0)
    if not own:
        grad_res, res_before, back_before = take(3)
    take(extra)
    hidden_ref, inner_ref = take(2)
    if own:
        grad_res = take(1)[0]
    if far:
        res_ref, back_ref = take(2)
    res_sum, back_sum = take(2)
    acts, hids = take(2), take(2)
    w_in, w_out, sems = take(3)
    steps = w_in.shape[0]
    half, width, experts = sz.half, sz.width, sz.experts
    step = pl.program_id(0)
    diag = iota((half, LANES), 0) == iota((half, LANES), 1)
    block = w_in.shape[2]
    wanted = own_copies(per_ring, block, in_own, out_own, w_in, w_out) if own else []
    if far:
        first_step = per_ring if own else 0
        wanted += far_copies(ring, per_ring, block, first_step, in_far, out_far, w_in, w_out)
    copies = [
        (at, pltpu.make_async_copy(source, target, sems.at[n]))
        for n, (at, source, target) in enumerate(wanted)
    ]

    @pl.when(step == 0)
    def _():
        for _at, copy in copies:
            copy.start()
        if not own:
            res_sum[...] = res_before[...]
            back_sum[...] = back_before[...]
            return
        for e in range(experts):
            at = e * half
            line = x_ref[at : at + 16, 0 : 3 * LANES].astype(F32)[0:1]
            gate = line[:, 0:LANES] + line[:, LANES : 2 * LANES] + line[:, 2 * LANES :]
            gate = jnp.sum(jnp.where(diag, gate, 0.0), axis=1, keepdims=True)
            grad_res[at : at + half, :] = (gate * dy_ref[e].astype(F32)).astype(BF)
        res_sum[...] = jnp.zeros_like(res_sum)
        back_sum[...] = jnp.zeros_like(back_sum)

    for at in range(steps):

        @pl.when(step == at)
        def _(at=at):
            for when, copy in copies:
                if when == at:
                    copy.wait()

    def work():
        chunk = x_ref.shape[0]
        in_ref, out_ref = w_in.at[step], w_out.at[step]
        tile = 256 if block % 256 == 0 else 128
        count = block // tile
        pieces = [slice(n * tile, (n + 1) * tile) for n in range(count)]
        spans = [slice(at, at + min(256, chunk)) for at in range(0, chunk, 256)]

        def enter(n, rows):
            acts[n % 2][rows, :] = dot_nn(x_ref[rows, :], in_ref[:, pieces[n]])
            hids[n % 2][rows, :] = dot_nt(grad_res[rows, :], out_ref[pieces[n], :])

        def activate(n, rows):
            for at in range(rows.start, rows.stop, 32):
                some = slice(at, at + 32)
                act, grad_hidden = acts[n % 2][some, :], hids[n % 2][some, :]
                bell = jnp.exp2(act * act * (-0.5 * LOG2_E))
                base = 1.0 + (ERFC_P * 2.0**-0.5) * jnp.abs(act)
                t = pl.reciprocal(base, approx=True)
                t = t * (2.0 - base * t)
                poly = 0.5 * ERFC_C[-1]
                for coefficient in ERFC_C[-2::-1]:
                    poly = poly * t + 0.5 * coefficient
                tail = poly * (t * bell)
                share = jnp.where(act >= 0.0, 1.0 - tail, tail)
                hidden_ref[some, pieces[n]] = (act * share).astype(BF)
                slope = share + act * (bell * 0.3989422804014327)
                inner_ref[some, pieces[n]] = (grad_hidden * slope).astype(BF)

        def leave(first, last, rows):
            part = slice(first * tile, last * tile)
            res_sum[rows, :] += dot_nn(hidden_ref[rows, part], out_ref[part, :])
            back_sum[rows, :] += dot_nt(inner_ref[rows, part], in_ref[:, part])

        for rows in spans:
            enter(0, rows)
        for n in range(count):
            for rows in spans:
                if n + 1 < count:
                    enter(n + 1, rows)
                elif n:
                    leave(0, n, rows)
                activate(n, rows)
        for rows in spans:
            leave(count - 1, count, rows)

    work()
    if not far:
        return

    @pl.when(step == steps - 1)
    def _():
        for e in range(experts):
            rows = slice(e * half, (e + 1) * half)
            res = res_sum[rows, :].astype(BF)
            res_ref[e] = res
            gate = jnp.sum(dy_ref[e].astype(F32) * res.astype(F32), axis=1, keepdims=True)
            line = jnp.sum(jnp.where(diag, gate, 0.0), axis=0, keepdims=True)
            pieces = [p.astype(F32) for p in split_three(line)]
            line = jnp.concatenate(pieces + [jnp.zeros((1, width - 3 * LANES), F32)], axis=1)
            back = jnp.where(iota((half, width), 0) == 0, line, back_sum[rows, :])
            back_ref[e] = back.astype(BF)


def hidden_block(hidden):
    return next(b for b in (768, 512, 384, 256, 128) if hidden % b == 0)


def call_experts(sz, c, ring, x, dy, own, far, before=(), res=None):
    width, half, chunk, experts = sz.width, sz.half, sz.chunk, sz.experts
    hidden = (own[0] if own else far[0][0]).shape[-1]
    block = hidden_block(hidden)
    per_ring = hidden // block
    steps = per_ring * ((1 if own else 0) + (ring - 1 if far else 0))
    last = bool(far) or ring == 1
    rows_spec = pl.BlockSpec((experts, half, width), lambda s: (0, 0, 0))
    flat_spec = pl.BlockSpec((chunk, width), lambda s: (0, 0))
    wide_spec = pl.BlockSpec((chunk, block), lambda s: (0, s))
    any_spec = pl.BlockSpec(memory_space=pl.ANY)
    weights = [*own, *(far[0] if far else []), *(far[1] if far else [])]
    tile = 256 if block % 256 == 0 else 128
    flat = lambda kind: jax.ShapeDtypeStruct((chunk, width), kind)
    rows = jax.ShapeDtypeStruct((experts, half, width), BF)
    both = jax.ShapeDtypeStruct((experts, 2 * half, width), BF)
    chunk_spec = pl.BlockSpec((experts, half, width), lambda s: (0, c, 0))
    wide = jax.ShapeDtypeStruct((chunk, steps * block), BF)
    out_specs, out_shape = [wide_spec, wide_spec], [wide, wide]
    if own:
        out_specs, out_shape = out_specs + [flat_spec], out_shape + [flat(BF)]
    sums = [pltpu.VMEM((chunk, width), F32)] * 2
    if last:
        out_specs, out_shape = out_specs + [chunk_spec, rows_spec], out_shape + [both, rows]
    else:
        out_specs, out_shape, sums = out_specs + [flat_spec] * 2, out_shape + [flat(F32)] * 2, []
    counts = (len(far[0]), len(far[1])) if far else (0, 0)
    given = [] if res is None else [res]
    return pl.pallas_call(
        functools.partial(
            expert_kernel, sz, ring, per_ring, bool(own), last, len(given), *counts
        ),
        grid=(steps,),
        in_specs=[flat_spec, pl.BlockSpec((experts, half, width), lambda s: (0, c, 0))]
        + [any_spec] * len(weights)
        + [flat_spec] * len(before)
        + [any_spec] * len(given),
        input_output_aliases={2 + len(weights) + len(before): 3} if given else {},
        out_specs=out_specs,
        out_shape=out_shape,
        scratch_shapes=sums
        + [pltpu.VMEM((chunk, tile), F32)] * 4
        + [
            pltpu.VMEM((steps, width, block), BF),
            pltpu.VMEM((steps, block, width), BF),
            pltpu.SemaphoreType.DMA((steps * (2 + sum(counts)),)),
        ],
        compiler_params=kernel_params(56),
        cost_estimate=SMALL_COST,
        name="experts",
    )(x, dy, *weights, *before, *given)


def weight_grad_kernel(
    x_one, x_two, grad_one, grad_two, hid_one, hid_two, inn_one, inn_two, _early, *refs
):
    x_t, grad_t = refs[-2:]
    count = (len(refs) - 2) // 2
    gi_refs, go_refs = refs[:count], refs[count : 2 * count]
    chunk = x_one.shape[0]

    @pl.when(pl.program_id(0) == 0)
    def _():
        x_t[:, :chunk] = x_one[...].T
        x_t[:, chunk:] = x_two[...].T
        grad_t[:, :chunk] = grad_one[...].T
        grad_t[:, chunk:] = grad_two[...].T

    grad_in = dot_nn(x_t[:, :chunk], inn_one[...]) + dot_nn(x_t[:, chunk:], inn_two[...])
    at = 0
    for ref in gi_refs:
        ref[...] = grad_in[at : at + ref.shape[0]].astype(ref.dtype)
        at += ref.shape[0]
    grad_out = dot_nn(grad_t[:, :chunk], hid_one[...]) + dot_nn(grad_t[:, chunk:], hid_two[...])
    grad_out = grad_out.T
    at = 0
    for ref in go_refs:
        ref[...] = grad_out[:, at : at + ref.shape[1]].astype(ref.dtype)
        at += ref.shape[1]


def call_weight_grads(sz, ring, hidden, far, flats, wides, early):
    width, chunk = sz.width, sz.chunk
    block = next(b for b in (512, 384, 256, 128) if hidden % b == 0)
    per_ring = hidden // block
    count = (ring - 1) * per_ring if far else per_ring
    flat_spec = pl.BlockSpec((chunk, width), lambda s: (0, 0))
    wide_spec = lambda first: pl.BlockSpec((chunk, block), lambda s: (0, first + s))
    wide_specs = [wide_spec(per_ring if far and whole else 0) for _array, whole in wides]
    if far:
        in_cuts, out_cuts = (width * 3 // 8, width * 5 // 8), (width // 3, width - width // 3)
        out_specs = [
            pl.BlockSpec((None, part, block), lambda s: (s // per_ring, 0, s % per_ring))
            for part in in_cuts
        ] + [
            pl.BlockSpec((None, block, part), lambda s: (s // per_ring, s % per_ring, 0))
            for part in out_cuts
        ]
        out_shape = [jax.ShapeDtypeStruct((ring - 1, part, hidden), BF) for part in in_cuts] + [
            jax.ShapeDtypeStruct((ring - 1, hidden, part), BF) for part in out_cuts
        ]
    else:
        out_specs = (
            pl.BlockSpec((width, block), lambda s: (0, s)),
            pl.BlockSpec((block, width), lambda s: (s, 0)),
        )
        out_shape = (
            jax.ShapeDtypeStruct((width, hidden), BF),
            jax.ShapeDtypeStruct((hidden, width), BF),
        )
    return pl.pallas_call(
        weight_grad_kernel,
        grid=(count,),
        in_specs=[flat_spec] * 4 + wide_specs + [pl.BlockSpec(memory_space=pl.ANY)],
        out_specs=out_specs,
        out_shape=out_shape,
        scratch_shapes=[pltpu.VMEM((width, 2 * chunk), BF), pltpu.VMEM((width, 2 * chunk), BF)],
        compiler_params=kernel_params(56),
        cost_estimate=pl.CostEstimate(
            flops=8 * chunk * width * block * count,
            bytes_accessed=8 * chunk * block * count + 8 * width * block * count,
            transcendentals=0,
        ),
        name="weight_grads",
    )(*flats, *(array for array, _whole in wides), early)


def combine_kernel(
    sz,
    back_one_ref,
    back_two_ref,
    slot_ref,
    slot_col_ref,
    gate_ref,
    routes_ref,
    proj_ref,
    tail_ref,
    dy_ref,
    after_ref,
    normed_ref,
    mixed_ref,
    _early,
    grad_after_ref,
    grad_mixed_ref,
    proj_grad_ref,
    small_ref,
    tail_t,
    from_router,
    branch_all,
):
    width, seq, rows, half, chunk = sz.width, sz.seq_pad, sz.rows, sz.half, sz.chunk
    step = pl.program_id(0)
    first = sz.experts

    @pl.when(step == 0)
    def _():
        tail_t[...] = tail_ref[...].astype(F32).T
        group = max(1, LANES // half)
        metas = []
        for ref in (back_one_ref, back_two_ref):
            for e0 in range(0, sz.experts, group):
                line = jnp.zeros((1, 3 * LANES), F32)
                for g in range(group):
                    at = (e0 + g) * half
                    one = ref[at : at + 16, 0 : 3 * LANES].astype(F32)
                    pieces = [one[:, m * LANES : (m + 1) * LANES] for m in range(3)]
                    if g:
                        pieces = [pltpu.roll(p, g * half, axis=1) for p in pieces]
                    line += jnp.concatenate([p[0:1] for p in pieces], axis=1)
                metas.append(line)
        part = iota((16, 2 * chunk), 0)
        coded = jnp.zeros((16, 2 * chunk), F32)
        for m in range(3):
            line = jnp.concatenate([x[:, m * LANES : (m + 1) * LANES] for x in metas], axis=1)
            coded = jnp.where(part == m, line, coded)
        coded = coded.astype(BF)
        grads = []
        for k in range(sz.choose):
            ids = iota((256, rows), 0)
            total = jnp.zeros((16, rows), F32)
            for start in range(0, 2 * chunk, 256):
                pick = ones_where(ids + start == slot_ref[k : k + 1]).astype(BF)
                total += dot_nn(coded[:, start : start + 256], pick)
            grads.append(jnp.sum(total, axis=0, keepdims=True))
        gates = [gate_ref[k : k + 1] for k in range(sz.choose)]
        mean_grad = functools.reduce(jnp.add, [g * v for g, v in zip(gates, grads)])
        kinds = iota((LANES, rows), 0)
        logits_grad = jnp.zeros((LANES, rows), F32)
        for k in range(sz.choose):
            chosen = gates[k] * (grads[k] - mean_grad)
            logits_grad = jnp.where(kinds == routes_ref[k : k + 1], chosen, logits_grad)
        logits_grad = logits_grad.astype(BF)
        small_ref[...] = dot_nn(logits_grad, normed_ref[...].reshape(rows, width))
        from_router[...] = dot_tn(logits_grad, tail_t[...].astype(BF))

    here = pl.ds(step * seq, seq)
    slot_col = slot_col_ref[here, :]
    upstream = from_router[here, :]
    for c, ref in enumerate((back_one_ref, back_two_ref)):
        ids = iota((seq, chunk), 1) + c * chunk
        pick = ids == slot_col[:, 0:1]
        for k in range(1, sz.choose):
            pick = pick | (ids == slot_col[:, k : k + 1])
        upstream += dot_nn(ones_where(pick).astype(BF), ref[...])
    normal, inv = norm_parts(after_ref[...])
    grad_after = dy_ref[...].astype(F32) + norm_back(
        upstream, tail_t[first + 2 : first + 3], normal, inv
    )
    live = iota((seq, 1), 0) < SEQ
    grad_after = jnp.where(live, grad_after, 0.0)
    upstream = jnp.where(live, upstream, 0.0)
    grad_after_ref[...] = grad_after
    branch = grad_after.astype(BF)
    branch_all[here, :] = branch
    grad_mixed_ref[...] = dot_nn(branch, proj_ref[...]).astype(BF)
    small_ref[first + 2 : first + 3, :] += jnp.sum(upstream * normal, axis=0, keepdims=True)
    small_ref[first + 3 : first + 4, :] += jnp.sum(upstream, axis=0, keepdims=True)

    @pl.when(step == sz.images - 1)
    def _():
        proj_grad_ref[...] = dot_tn(
            branch_all[...], mixed_ref[...].reshape(rows, width)
        ).astype(BF)


def call_combine(
    sz,
    back_one,
    back_two,
    slots,
    slot_col,
    gates,
    routes_row,
    packed,
    dy,
    attended,
    normed,
    mixed,
    early,
):
    images, seq, width, rows = sz.images, sz.seq_pad, sz.width, sz.rows
    per_image = lambda size: pl.BlockSpec((None, seq, size), lambda i: (i, 0, 0))
    whole = lambda *shape: pl.BlockSpec(shape, lambda i: (0,) * len(shape))
    return pl.pallas_call(
        functools.partial(combine_kernel, sz),
        grid=(images,),
        in_specs=[
            whole(sz.chunk, width),
            whole(sz.chunk, width),
            whole(8, rows),
            whole(rows, LANES),
            whole(8, rows),
            whole(8, rows),
            pl.BlockSpec((width, width), lambda i: (0, 1)),
            pl.BlockSpec((width, LANES), lambda i: (0, 2 * width // LANES)),
            per_image(width),
            per_image(width),
            whole(images, seq, width),
            whole(images, seq, width),
            pl.BlockSpec(memory_space=pl.ANY),
        ],
        out_specs=(
            per_image(width),
            per_image(width),
            whole(width, width),
            whole(LANES, width),
        ),
        out_shape=(
            jax.ShapeDtypeStruct((images, seq, width), F32),
            jax.ShapeDtypeStruct((images, seq, width), BF),
            jax.ShapeDtypeStruct((width, width), BF),
            jax.ShapeDtypeStruct((LANES, width), F32),
        ),
        scratch_shapes=[
            pltpu.VMEM((LANES, width), F32),
            pltpu.VMEM((rows, width), F32),
            pltpu.VMEM((rows, width), BF),
        ],
        compiler_params=kernel_params(56),
        cost_estimate=pl.CostEstimate(
            flops=4 * rows * width * width + 4 * rows * sz.chunk * width,
            bytes_accessed=rows * width * 16 + 4 * sz.chunk * width + 4 * width * width,
            transcendentals=0,
        ),
        name="combine",
    )(
        back_one,
        back_two,
        slots,
        slot_col,
        gates,
        routes_row,
        packed[1],
        packed[1],
        dy,
        attended,
        normed,
        mixed,
        early,
    )


def attend_back_kernel(
    sz,
    tok_ref,
    w_one_ref,
    w_two_ref,
    qkv_ref,
    lse_ref,
    grad_mixed_ref,
    grad_after_ref,
    proj_grad_ref,
    small_ref,
    core_ref,
    _early,
    tok_grad_ref,
    *refs,
):
    packed_refs = refs[:-4]
    tail_t, normed_all, grad_all, small_sum = refs[-4:]
    width, seq, rows = sz.width, sz.seq_pad, sz.rows
    step = pl.program_id(0)
    first = sz.experts

    @pl.when(step == 0)
    def _():
        tail_t[...] = w_two_ref[:, 2 * width :].astype(F32).T
        small_sum[...] = small_ref[...]

    here = pl.ds(step * seq, seq)
    gain, bias = tail_t[first : first + 1], tail_t[first + 1 : first + 2]
    normal, inv = norm_parts(tok_ref[...].astype(F32))
    normed_all[here, :] = (normal * gain + bias).astype(BF)
    key_ok = iota((seq, seq), 0) < SEQ
    pair_lane = iota((1, LANES), 1) // HEAD
    for j in range(HEADS // 2):
        at = j * LANES
        q = qkv_ref[:, at : at + LANES]
        key = qkv_ref[:, width + at : width + at + LANES]
        val = qkv_ref[:, 2 * width + at : 2 * width + at + LANES]
        grad = grad_mixed_ref[:, at : at + LANES]
        sum_q = jnp.zeros((seq, LANES), F32)
        sum_k = jnp.zeros((seq, LANES), F32)
        sum_v = jnp.zeros((seq, LANES), F32)
        for a in range(2):
            own = ones_where(pair_lane == a).astype(BF)
            scaled = own * HEAD**-0.5
            q_own, grad_own = q * scaled, grad * own
            scores = dot_nt(key, q_own)
            lse = lse_ref[2 * j + a : 2 * j + a + 1, :]
            probs = jnp.where(key_ok, jnp.exp(scores - lse), 0.0)
            grad_probs = dot_nt(val, grad_own)
            sum_v += dot_nn(probs.astype(BF), grad_own)
            delta = jnp.sum(grad_probs * probs, axis=0, keepdims=True)
            grad_scores = (probs * (grad_probs - delta)).astype(BF)
            sum_q += dot_tn(grad_scores, key * scaled)
            sum_k += dot_nn(grad_scores, q_own)
        grad_all[here, at : at + LANES] = sum_q.astype(BF)
        grad_all[here, width + at : width + at + LANES] = sum_k.astype(BF)
        grad_all[here, 2 * width + at : 2 * width + at + LANES] = sum_v.astype(BF)
    upstream = dot_nt(grad_all[here, : 2 * width], w_one_ref[...])
    upstream += dot_nt(grad_all[here, 2 * width :], w_two_ref[:, :width])
    tok_grad_ref[...] = grad_after_ref[...] + norm_back(upstream, gain, normal, inv)
    small_sum[first : first + 1, :] += jnp.sum(upstream * normal, axis=0, keepdims=True)
    small_sum[first + 1 : first + 2, :] += jnp.sum(upstream, axis=0, keepdims=True)

    @pl.when(step == sz.images - 1)
    def _():
        parts = (
            dot_tn(normed_all[...], grad_all[...]),
            proj_grad_ref[...].astype(F32),
            small_sum[...].T,
        )
        if len(packed_refs) == 1:
            at = 0
            for part in parts:
                size = part.shape[1]
                packed_refs[0][:, at : at + size] = part.astype(BF)
                at += size
            return
        keep_one, send_one, keep_two, send_two = packed_refs
        n_dp, ring, shard, _ = keep_one.shape
        first_core = core_ref[0] == 0

        def put(keep, send, at, part, part_lanes):
            size = part_lanes.stop - part_lanes.start
            for d in range(n_dp):
                for r in range(ring):
                    row = (d * ring + r) * 2 * shard
                    zero = part[row : row + shard, part_lanes]
                    one = part[row + shard : row + 2 * shard, part_lanes]
                    place = (d, r) if keep is keep_one else (r, d)
                    keep[(*place, slice(None), slice(at, at + size))] = jnp.where(
                        first_core, zero, one
                    ).astype(BF)
                    send[(*place, slice(None), slice(at, at + size))] = jnp.where(
                        first_core, one, zero
                    ).astype(BF)

        put(keep_one, send_one, 0, parts[0], slice(0, 2 * width))
        put(keep_two, send_two, 0, parts[0], slice(2 * width, 3 * width))
        put(keep_two, send_two, width, parts[1], slice(0, width))
        put(keep_two, send_two, 2 * width, parts[2], slice(0, parts[2].shape[1]))


def call_attend_back(
    sz, tok, packed, qkv, lse, grad_mixed, grad_after, proj_grad, small, core, early, out_dims
):
    images, seq, width, rows = sz.images, sz.seq_pad, sz.width, sz.rows
    per_image = lambda size: pl.BlockSpec((None, seq, size), lambda i: (i, 0, 0))
    lse_spec = pl.BlockSpec((None, 16, seq), lambda i: (i, 0, 0))
    whole = lambda *shape: pl.BlockSpec(shape, lambda i: (0,) * len(shape))
    return pl.pallas_call(
        functools.partial(attend_back_kernel, sz),
        grid=(images,),
        in_specs=[
            per_image(width),
            whole(width, sz.part_one),
            whole(width, sz.part_two),
            per_image(3 * width),
            lse_spec,
            per_image(width),
            per_image(width),
            whole(width, width),
            whole(LANES, width),
            pl.BlockSpec(memory_space=pltpu.SMEM),
            pl.BlockSpec(memory_space=pl.ANY),
        ],
        out_specs=(per_image(width), *(whole(*dims) for dims in out_dims)),
        out_shape=(
            jax.ShapeDtypeStruct((images, seq, width), F32),
            *(jax.ShapeDtypeStruct(dims, BF) for dims in out_dims),
        ),
        scratch_shapes=[
            pltpu.VMEM((LANES, width), F32),
            pltpu.VMEM((rows, width), BF),
            pltpu.VMEM((rows, 3 * width), BF),
            pltpu.VMEM((LANES, width), F32),
        ],
        compiler_params=kernel_params(56),
        cost_estimate=pl.CostEstimate(
            flops=12 * rows * width * width + 10 * rows * seq * width,
            bytes_accessed=4 * width * sz.packed + rows * width * 18,
            transcendentals=rows * seq * HEADS,
        ),
        name="attend_back",
    )(tok, *packed, qkv, lse, grad_mixed, grad_after, proj_grad, small, core, early)


def output_kernel(sz, res_ref, slot_col_ref, gate_col_ref, after_ref, out_ref):
    seq, chunk = sz.seq_pad, sz.chunk
    here = pl.ds(pl.program_id(0) * seq, seq)
    slot_col = slot_col_ref[here, :]
    gate_col = gate_col_ref[here, :]
    moe = jnp.zeros((seq, sz.width), F32)
    for k in range(sz.choose):
        rows = jnp.zeros((seq, sz.width), F32)
        for c in range(2):
            ids = iota((seq, chunk), 1) + c * chunk
            res = res_ref[:, c * sz.half : (c + 1) * sz.half, :].reshape(chunk, sz.width)
            rows += dot_nn(ones_where(ids == slot_col[:, k : k + 1]).astype(BF), res)
        moe += gate_col[:, k : k + 1] * rows
    out_ref[...] = (after_ref[...] + moe).astype(BF)


def call_output(sz, res, slot_col, gate_col, after):
    images, seq, width, rows = sz.images, sz.seq_pad, sz.width, sz.rows
    per_image = pl.BlockSpec((None, seq, width), lambda i: (i, 0, 0))
    whole = lambda *shape: pl.BlockSpec(shape, lambda i: (0,) * len(shape))
    return pl.pallas_call(
        functools.partial(output_kernel, sz),
        grid=(images,),
        in_specs=[
            whole(sz.experts, 2 * sz.half, width),
            whole(rows, LANES),
            whole(rows, LANES),
            per_image,
        ],
        out_specs=per_image,
        out_shape=jax.ShapeDtypeStruct((images, seq, width), BF),
        compiler_params=kernel_params(24),
        cost_estimate=SMALL_COST,
        name="output",
    )(res, slot_col, gate_col, after)


def adam_update(weight, gradient, moment_one, moment_two, clip_scale, rate_val, decay_val):
    clipped = gradient * clip_scale
    first_new = BETA_ONE * moment_one + (1.0 - BETA_ONE) * clipped
    second_new = BETA_TWO * moment_two + (1.0 - BETA_TWO) * clipped * clipped
    first_hat = first_new / (1.0 - BETA_ONE**STEP)
    second_hat = second_new / (1.0 - BETA_TWO**STEP)
    return (
        first_new,
        second_new,
        weight - rate_val * (first_hat / (jnp.sqrt(second_hat) + ADAM_EPS) + decay_val * weight),
    )


def exchange(array):
    return lax.all_to_all(array, GROUP, split_axis=0, concat_axis=0, tiled=True)


class Gather:
    def __init__(self, array):
        self.rank, self.done, self.array = {}, [], array
        for axis in ALL:
            for bit in reversed(range(lax.axis_size(axis).bit_length() - 1)):
                self.rank[axis, bit] = len(self.rank)

    def bits(self, axis):
        return [key for key in self.rank if key[0] == axis]

    def advance(self, keys):
        for key in keys:
            self.double(*key)
        return self.array

    def part(self, lanes):
        other = Gather(self.array[..., lanes])
        other.done = list(self.done)
        return other

    def double(self, axis, bit):
        array, flip = self.array, 1 << bit
        other = lax.ppermute(array, axis, [(s, s ^ flip) for s in range(lax.axis_size(axis))])
        at = sum(self.rank[key] < self.rank[axis, bit] for key in self.done)
        here = (lax.axis_index(axis) >> bit) & 1
        side = lax.broadcasted_iota(jnp.int32, (1,) * at + (2,) + (1,) * (array.ndim - at), at)
        self.array = jnp.where(side == here, jnp.expand_dims(array, at), jnp.expand_dims(other, at))
        self.done.append((axis, bit))

    def wait(self, *others):
        self.array = after(self.array, *others)


def scatter_ring(grads, axis):
    count, here = lax.axis_size(axis), lax.axis_index(axis)
    pick = lambda at: lax.dynamic_index_in_dim(grads, at % count, 0, keepdims=False)
    total = pick(here).astype(F32)
    for r in range(1, count):
        ahead = [(s, (s + r) % count) for s in range(count)]
        total += lax.ppermute(pick(here + r), axis, ahead).astype(F32)
    return total


def after(array, *others):
    return lax.optimization_barrier((array, *others))[0]


def on_device(
    tokens,
    out_grad,
    routes,
    slot_order,
    norm_params,
    qkv_weight,
    proj_weight,
    router_weight,
    inner_weight,
    outer_weight,
    norm_moment,
    norm_second,
    qkv_moment,
    qkv_second,
    proj_moment,
    proj_second,
    router_moment,
    router_second,
    inner_moment,
    inner_second,
    outer_moment,
    outer_second,
):
    tok_count, width = tokens.shape
    choose = routes.shape[1]
    experts = router_weight.shape[1]
    sz = Sizes(tok_count, width, choose, experts)
    images, seq, rows = sz.images, sz.seq_pad, sz.rows
    ring = lax.axis_size("row")
    n_dp, n_col = lax.axis_size("dp"), lax.axis_size("col")
    shard = qkv_weight.shape[0]

    gather = Gather(
        jnp.concatenate(
            [
                qkv_weight.astype(BF).reshape(shard, 3 * width),
                proj_weight.astype(BF),
                router_weight.astype(BF),
                norm_params.astype(BF),
                jnp.zeros((shard, sz.packed - 4 * width - experts - 4), BF),
            ],
            axis=1,
        )
    )
    in_own = lax.optimization_barrier(inner_weight[0].astype(BF))
    out_own = lax.optimization_barrier(outer_weight[0].astype(BF))

    def from_ahead(array, r):
        return lax.ppermute(array, "row", [(s, (s - r) % ring) for s in range(ring)])

    def to_ahead(array, r):
        return lax.ppermute(array, "row", [(s, (s + r) % ring) for s in range(ring)])

    def from_row(array):
        if ring == 1:
            return array[None]
        return jnp.stack([from_ahead(array, r) for r in range(1, ring)])

    cut = width // 4
    in_top = [from_row(in_own[:cut]), from_row(in_own[cut : 2 * cut])]

    def pad_rows(array):
        array = array.reshape(images, SEQ, array.shape[1])
        return jnp.pad(array, ((0, 0), (0, seq - SEQ), (0, 0)))

    tok_pad, dy_pad = pad_rows(tokens), pad_rows(out_grad)
    order = slot_order[0]
    order = (order % choose) * rows + order // choose
    order = jnp.pad(order, (0, sz.rank - sz.pairs), constant_values=-1).reshape(1, sz.rank)
    fill = ((0, 0), (0, rows - tok_count))
    routes_flat = jnp.pad(routes.T, fill, constant_values=-1).reshape(1, choose * rows)
    dy_flat = jnp.pad(out_grad, ((0, rows - tok_count), (0, 0)))
    flat_slots, dy_send = call_slots(sz, order, routes_flat, dy_flat)
    slots = jnp.pad(
        flat_slots[:, :tok_count].reshape(8, images, SEQ),
        ((0, 0), (0, 0), (0, seq - SEQ)),
        constant_values=-1,
    ).reshape(8, rows)
    slot_col = jnp.pad(slots.T, ((0, 0), (0, LANES - 8)))
    routes_row = jnp.pad(
        slots[choose : 2 * choose], ((0, 8 - choose), (0, 0)), constant_values=-1
    )
    dp_bits, row_bits, col_bits = gather.bits("dp"), gather.bits("row"), gather.bits("col")
    gather.advance(dp_bits[:-1])
    gather.wait(flat_slots, in_top[0])
    part_one = gather.part(slice(0, sz.part_one))
    part_two = gather.part(slice(sz.part_one, sz.packed))
    part_one.advance(dp_bits[-1:])
    part_two.advance(dp_bits[-1:])
    dy_there = exchange(after(dy_send, part_one.array, part_two.array, in_top[1]))
    one_row = part_one.advance(row_bits)
    part_one.wait(tok_pad, out_own)
    part_one = part_one.advance(col_bits)
    part_two = part_two.advance(row_bits + col_bits)
    packed = (part_one.reshape(width, sz.part_one), part_two.reshape(width, sz.part_two))
    in_far = [*in_top, from_row(after(in_own[2 * cut :], one_row))]
    cut = out_own.shape[0] * 9 // 32 // 16 * 16
    out_far = [from_row(after(out_own[:cut], one_row)), from_row(out_own[cut:])]

    qkv, lse, mixed, attended, normed, gates, gate_col, send_one, send_two = call_attend(
        sz, tok_pad, packed, routes_row, slots
    )

    def exchange_rows(array):
        return exchange(array.reshape(experts, sz.half, width)).reshape(sz.chunk, width)

    x_one = exchange_rows(after(send_one, dy_there, in_far[2], out_far[0]))
    x_two = exchange_rows(after(send_two, x_one, out_far[1], dy_pad, slot_col))
    own, far = [in_own, out_own], [in_far, out_far] if ring > 1 else None
    hidden_one, inner_one, grad_one, res_one, back_one = call_experts(
        sz, 0, ring, x_one, dy_there, own, far
    )
    hidden_two, inner_two, grad_two, res_both, back_two = call_experts(
        sz, 1, ring, x_two, dy_there, own, far, res=res_one
    )
    wides = [(array, True) for array in (hidden_one, hidden_two, inner_one, inner_two)]
    flats = (x_one, x_two, grad_one, grad_two)
    first_back = back_two
    back_one = exchange(back_one).reshape(sz.chunk, width)
    back_two = exchange(back_two).reshape(sz.chunk, width)
    hidden = in_own.shape[1]
    away = None
    if ring > 1:
        away = call_weight_grads(sz, ring, hidden, True, flats, wides, first_back)
    in_grad, out_grad_own = call_weight_grads(
        sz, ring, hidden, False, flats, wides, first_back if away is None else away[0]
    )
    kept_grads = (in_grad, out_grad_own)
    in_sent, out_sent = [[], []], [[], []]
    if ring > 1:
        send = lambda array: [to_ahead(part, r + 1) for r, part in enumerate(array)]
        in_sent, out_sent = [send(away[0]), send(away[1])], [send(away[2]), send(away[3])]
        for top, low in zip(*in_sent):
            in_grad = in_grad.astype(F32) + jnp.concatenate([top, low]).astype(F32)
        for top, low in zip(*out_sent):
            out_grad_own = out_grad_own.astype(F32) + jnp.concatenate([top, low], axis=1).astype(F32)
    res = exchange(after(res_both, *kept_grads, *in_sent[0]))

    grad_after, grad_mixed, proj_grad, small = call_combine(
        sz,
        back_one,
        back_two,
        slots,
        slot_col,
        gates,
        routes_row,
        packed,
        dy_pad,
        attended,
        normed,
        mixed,
        kept_grads[0],
    )
    direct = shard % 8 == 0 and n_col == 2
    one_dims = (n_dp, ring, shard, sz.part_one)
    two_dims = (ring, n_dp, shard, sz.part_two)
    core = lax.axis_index("col")
    tok_grad, *packed_grads = call_attend_back(
        sz,
        tok_pad,
        packed,
        qkv,
        lse,
        grad_mixed,
        grad_after,
        proj_grad,
        small,
        core.astype(jnp.int32).reshape(1),
        kept_grads[0],
        [one_dims, one_dims, two_dims, two_dims] if direct else [(width, sz.packed)],
    )
    block_out = call_output(sz, res, slot_col, gate_col, attended)

    if direct:
        keep_one, send_one, keep_two, send_two = packed_grads
        swap = lambda sent: lax.ppermute(sent, "col", [(0, 1), (1, 0)]).astype(F32)
        sum_one = keep_one.astype(F32) + swap(after(send_one, *in_sent[1], *out_sent[0]))
        sum_two = keep_two.astype(F32) + swap(after(send_two, *in_sent[1], *out_sent[0]))
    else:
        grads = packed_grads[0].reshape(n_dp, ring, n_col, shard, sz.packed)
        grads = scatter_ring(grads.transpose(2, 0, 1, 3, 4), "col")
        sum_one = grads[..., : sz.part_one]
        sum_two = grads[..., sz.part_one :].transpose(1, 0, 2, 3)

    def scatter_dp(grads):
        return lax.all_to_all(grads.astype(BF), "dp", split_axis=0, concat_axis=0, tiled=True)

    sum_one = jnp.sum(scatter_dp(after(sum_one, res)).astype(F32), axis=0)
    sum_two = scatter_ring(after(sum_two.astype(BF), *out_sent[1], block_out), "row")
    block_out = block_out[:, :SEQ].reshape(tok_count, width)
    tok_grad = tok_grad[:, :SEQ].reshape(tok_count, width)
    parts = scatter_dp(after(sum_two, sum_one, block_out, tok_grad))
    share_one = scatter_ring(sum_one.astype(BF), "row")
    share_two = jnp.sum(parts.astype(F32), axis=0)
    share = jnp.concatenate([share_one, share_two], axis=1)
    qkv_share = share[:, : 3 * width].reshape(shard, 3, width)
    proj_share = share[:, 3 * width : 4 * width]
    router_share = share[:, 4 * width : 4 * width + experts]
    norm_share = share[:, 4 * width + experts : 4 * width + experts + 4]

    in_grad, out_grad_own = in_grad.astype(F32), out_grad_own.astype(F32)
    local_square = (
        jnp.sum(share * share) + jnp.sum(in_grad * in_grad) + jnp.sum(out_grad_own * out_grad_own)
    )
    count = n_dp * ring * n_col
    squares = lax.all_to_all(
        jnp.broadcast_to(local_square, (count, 1, LANES)), ALL, split_axis=0, concat_axis=0, tiled=True
    )
    square_sum = jnp.sum(squares[:, 0, 0])
    grad_norm = jnp.sqrt(square_sum)
    clip_scale = jnp.minimum(1.0, CLIP_NORM / (grad_norm + 1e-06))
    outs = [
        block_out,
        tok_grad,
        grad_norm,
    ]
    outs += adam_update(
        norm_params, norm_share, norm_moment, norm_second, clip_scale, RATE_NORM, 0.0
    )
    for weight, grad, moment, second in (
        (qkv_weight, qkv_share, qkv_moment, qkv_second),
        (proj_weight, proj_share, proj_moment, proj_second),
        (router_weight, router_share, router_moment, router_second),
        (inner_weight, in_grad[None], inner_moment, inner_second),
        (outer_weight, out_grad_own[None], outer_moment, outer_second),
    ):
        outs += adam_update(weight, grad, moment, second, clip_scale, RATE_MATRIX, DECAY_MATRIX)
    return tuple(outs)


def solution(mesh):
    rows = P(ALL, None)
    cube = P(ALL, None, None)
    inner = P(GROUP, None, "row")
    outer = P(GROUP, "row", None)
    return jax.shard_map(
        on_device,
        mesh=mesh,
        in_specs=(rows,) * 5
        + (cube, rows, rows, inner, outer)
        + (rows, rows, cube, cube, rows, rows, rows, rows, inner, inner, outer, outer),
        out_specs=(rows, rows, P())
        + (rows,) * 3
        + (cube,) * 3
        + (rows,) * 6
        + (inner,) * 3
        + (outer,) * 3,
        check_vma=False,
    )
```

```python
import functools

import jax
import jax.numpy as jnp
from jax import lax
from jax.experimental import pallas as pl
from jax.experimental.pallas import tpu as pltpu
from jax.sharding import PartitionSpec as P

HEADS = 12
HEAD = 64
SEQ = 197
STEP = 10

NORM_EPS = 1e-06
CLIP_NORM = 1.0
BETA_ONE = 0.9
BETA_TWO = 0.999
ADAM_EPS = 1e-08
RATE_MATRIX = 0.08
RATE_NORM = 0.4
DECAY_MATRIX = 0.1

LANES = 128
MIB = 1024 * 1024
SMALL_COST = pl.CostEstimate(flops=1024, bytes_accessed=1024, transcendentals=0)
ALL = ("dp", "row", "col")
GROUP = ("dp", "col")
BF = jnp.bfloat16
F32 = jnp.float32

ERFC_P = 0.39
LOG2_E = 1.4426950408889634
ERFC_C = (
    0.23532534336933997,
    0.09138763496502661,
    0.649561341403834,
    -0.6354026835533981,
    0.8866658487971544,
    -0.2275374866853928,
)


def round_up(value, unit):
    return -(-value // unit) * unit


def dot_nn(a, b):
    return lax.dot_general(a, b, (((1,), (0,)), ((), ())), preferred_element_type=F32)


def dot_nt(a, b):
    return lax.dot_general(a, b, (((1,), (1,)), ((), ())), preferred_element_type=F32)


def dot_tn(a, b):
    return lax.dot_general(a, b, (((0,), (0,)), ((), ())), preferred_element_type=F32)


def iota(shape, dim):
    return lax.broadcasted_iota(jnp.int32, shape, dim)


def ones_where(cond):
    return jnp.where(cond, 1.0, 0.0)


def split_three(value):
    high = value.astype(BF)
    rest = value - high.astype(F32)
    middle = rest.astype(BF)
    low = (rest - middle.astype(F32)).astype(BF)
    return high, middle, low


def kernel_params(mebibytes):
    return pltpu.CompilerParams(vmem_limit_bytes=mebibytes * MIB)


def norm_parts(rows):
    mean_val = jnp.mean(rows, axis=-1, keepdims=True)
    centred = rows - mean_val
    spread_val = jnp.mean(centred * centred, axis=-1, keepdims=True)
    inv = lax.rsqrt(spread_val + NORM_EPS)
    return centred * inv, inv


def norm_back(upstream, gain, normal, inv):
    scaled = upstream * gain
    return inv * (
        scaled
        - jnp.mean(scaled, axis=-1, keepdims=True)
        - normal * jnp.mean(scaled * normal, axis=-1, keepdims=True)
    )


class Sizes:
    def __init__(self, tok_count, width, choose, experts):
        self.tok = tok_count
        self.width = width
        self.choose = choose
        self.experts = experts
        self.pairs = tok_count * choose
        self.cap = max(2, (5 * self.pairs + 4 * experts - 1) // (4 * experts))
        half = 16
        while 2 * (half - 1) < self.cap:
            half *= 2
        self.half = half
        self.chunk = experts * half
        self.images = tok_count // SEQ
        self.seq_pad = round_up(SEQ, 32)
        self.rows = self.images * self.seq_pad
        self.rank = round_up(self.pairs, 256)
        self.packed = round_up(4 * width + experts + 4, LANES)
        self.part_one = 2 * width
        self.part_two = self.packed - self.part_one


def slots_kernel(sz, order_ref, routes_ref, dy_ref, slot_ref, send_ref, hot_ref):
    rows, rank, experts, half, chunk = sz.rows, sz.rank, sz.experts, sz.half, sz.chunk
    order = order_ref[...]
    ranked = jnp.zeros((experts, rank), F32)
    for start in range(0, sz.choose * rows, 256):
        size = min(256, sz.choose * rows - start)
        hit = ones_where(order == iota((size, rank), 0) + start).astype(BF)
        hot_ref[start : start + size, :] = hit
        kind = ones_where(
            routes_ref[0:1, start : start + size] == iota((experts, size), 0)
        ).astype(BF)
        ranked += dot_nn(kind, hit)
    ranked_low = ranked.astype(BF)
    before = jnp.zeros((experts, rank), F32)
    for start in range(0, rank, 256):
        earlier = ones_where(iota((256, rank), 0) + start < iota((256, rank), 1)).astype(BF)
        before += dot_nn(ranked_low[:, start : start + 256], earlier)
    position = jnp.sum(before * ranked, axis=0, keepdims=True)
    named = jnp.sum(ranked * iota((experts, rank), 0).astype(F32), axis=0, keepdims=True)
    real = jnp.sum(ranked, axis=0, keepdims=True)
    kept = real * ones_where(position < sz.cap)
    second = ones_where(position >= half - 1)
    row_in = position + 1.0 - second * (half - 1)
    row_in = jnp.where(kept > 0.5, row_in, 0.0)
    part = iota((16, rank), 0)
    codes = jnp.where(
        part == 0, named, jnp.where(part == 1, row_in, jnp.where(part == 2, second, kept))
    )
    codes = jnp.where(part < 4, codes, 0.0).astype(BF)
    wide = iota((LANES, rows), 0)
    table = jnp.full((LANES, rows), -1.0, F32)
    for k in range(sz.choose):
        route = routes_ref[0:1, k * rows : (k + 1) * rows].astype(F32)
        table = jnp.where(wide == sz.choose + k, route, table)
    for k in range(sz.choose):
        back = dot_nt(codes, hot_ref[k * rows : (k + 1) * rows, :])
        slot = jnp.where(
            back[3:4] > 0.5, back[2:3] * chunk + back[0:1] * half + back[1:2], -1.0
        )
        table = jnp.where(wide == k, slot, table)
    slot_ref[...] = table[0:8].astype(jnp.int32)
    slots = slot_ref[...]
    block = min(256, chunk)
    dy = dy_ref[...]
    for c in range(2):
        for start in range(0, chunk, block):
            ids = iota((block, rows), 0) + (c * chunk + start)
            pick = ids == slots[0:1]
            for k in range(1, sz.choose):
                pick = pick | (ids == slots[k : k + 1])
            moved = dot_nn(ones_where(pick).astype(BF), dy).astype(BF)
            send_ref[start // half : (start + block) // half, c * half : (c + 1) * half] = (
                moved.reshape(block // half, half, sz.width)
            )


def call_slots(sz, order, routes_row, dy):
    return pl.pallas_call(
        functools.partial(slots_kernel, sz),
        out_shape=(
            jax.ShapeDtypeStruct((8, sz.rows), jnp.int32),
            jax.ShapeDtypeStruct((sz.experts, 2 * sz.half, sz.width), BF),
        ),
        scratch_shapes=[pltpu.VMEM((sz.choose * sz.rows, sz.rank), BF)],
        compiler_params=kernel_params(56),
        cost_estimate=SMALL_COST,
        name="slots",
    )(order, routes_row, dy)


def attend_kernel(
    sz,
    tok_ref,
    w_one_ref,
    w_two_ref,
    routes_ref,
    slot_ref,
    qkv_ref,
    lse_ref,
    mixed_ref,
    after_ref,
    normed_ref,
    gate_ref,
    gate_col_ref,
    send_one_ref,
    send_two_ref,
    normed_all,
    tail_t,
):
    width, seq, rows = sz.width, sz.seq_pad, sz.rows
    step = pl.program_id(0)

    @pl.when(step == 0)
    def _():
        tail_t[...] = w_two_ref[:, 2 * width :].astype(F32).T

    first = sz.experts
    gain_one, bias_one = tail_t[first : first + 1], tail_t[first + 1 : first + 2]
    gain_two, bias_two = tail_t[first + 2 : first + 3], tail_t[first + 3 : first + 4]
    tok = tok_ref[...].astype(F32)
    normal, _ = norm_parts(tok)
    normed = (normal * gain_one + bias_one).astype(BF)
    qkv_ref[:, : 2 * width] = dot_nn(normed, w_one_ref[...]).astype(BF)
    qkv_ref[:, 2 * width :] = dot_nn(normed, w_two_ref[:, :width]).astype(BF)
    lane = iota((seq, LANES), 1)
    key_ok = iota((seq, seq), 0) < SEQ
    pair_lane = iota((1, LANES), 1) // HEAD
    for j in range(HEADS // 2):
        at = j * LANES
        q = qkv_ref[:, at : at + LANES]
        key = qkv_ref[:, width + at : width + at + LANES]
        val = qkv_ref[:, 2 * width + at : 2 * width + at + LANES]
        outs = []
        for a in range(2):
            own = jnp.where(pair_lane == a, HEAD**-0.5, 0.0).astype(BF)
            scores = jnp.where(key_ok, dot_nt(key, q * own), -1e30)
            top = jnp.max(scores, axis=0, keepdims=True)
            raised = jnp.exp(scores - top)
            total = jnp.sum(raised, axis=0, keepdims=True)
            probs = (raised * (1.0 / total)).astype(BF)
            outs.append(dot_tn(probs, val))
            lse_ref[2 * j + a : 2 * j + a + 1, :] = top + jnp.log(total)
        mixed_ref[:, at : at + LANES] = jnp.where(lane < HEAD, outs[0], outs[1]).astype(BF)
    after = tok + dot_nt(mixed_ref[...], w_two_ref[:, width : 2 * width])
    after_ref[...] = after
    normal, _ = norm_parts(after)
    normed_two = (normal * gain_two + bias_two).astype(BF)
    normed_ref[...] = normed_two
    normed_all[pl.ds(step * seq, seq), :] = normed_two

    @pl.when(step == sz.images - 1)
    def _():
        normed_two = normed_all[...]
        logits = dot_nt(tail_t[...].astype(BF), normed_two)
        kinds = iota((LANES, rows), 0)
        chosen = [
            jnp.sum(jnp.where(kinds == routes_ref[k : k + 1], logits, 0.0), axis=0, keepdims=True)
            for k in range(sz.choose)
        ]
        top = functools.reduce(jnp.maximum, chosen)
        raised = [jnp.exp(c - top) for c in chosen]
        total = functools.reduce(jnp.add, raised)
        gates = [r / total for r in raised]
        wide = jnp.zeros((LANES, rows), F32)
        for k in range(sz.choose):
            wide = jnp.where(kinds == k, gates[k], wide)
        gate_ref[...] = wide[0:8]
        gate_col_ref[...] = wide.T
        half, chunk = sz.half, sz.chunk
        part = iota((16, rows), 0)
        coded = []
        for k in range(sz.choose):
            pieces = split_three(gates[k])
            table = jnp.zeros((16, rows), F32)
            for m in range(3):
                table = jnp.where(part == m, pieces[m].astype(F32), table)
            coded.append(table.astype(BF))
        block = min(256, chunk)
        for c, out_ref in enumerate((send_one_ref, send_two_ref)):
            for start in range(0, chunk, block):
                ids = iota((block, rows), 0) + (c * chunk + start)
                picks = [
                    ones_where(ids == slot_ref[k : k + 1]).astype(BF) for k in range(sz.choose)
                ]
                moved = dot_nn(functools.reduce(jnp.add, picks), normed_two)
                meta = functools.reduce(
                    jnp.add, [dot_nt(coded[k], picks[k]) for k in range(sz.choose)]
                )
                for e in range(block // half):
                    base, shift = (e * half) // LANES * LANES, (e * half) % LANES
                    near = meta[0:8, base : base + LANES] if block >= LANES else meta[0:8]
                    if shift:
                        near = pltpu.roll(near, LANES - shift, axis=1)
                    line = jnp.concatenate(
                        [near[0:1], near[1:2], near[2:3], jnp.zeros((1, width - 3 * LANES), F32)],
                        axis=1,
                    )
                    body = moved[e * half : (e + 1) * half]
                    body = jnp.where(iota((half, width), 0) == 0, line, body)
                    at = start + e * half
                    out_ref[at : at + half, :] = body.astype(BF)


def call_attend(sz, tok, packed, routes_row, slots):
    images, seq, width, rows = sz.images, sz.seq_pad, sz.width, sz.rows
    per_image = lambda size: pl.BlockSpec((None, seq, size), lambda i: (i, 0, 0))
    lse_spec = pl.BlockSpec((None, 16, seq), lambda i: (i, 0, 0))
    whole = lambda *shape: pl.BlockSpec(shape, lambda i: (0,) * len(shape))
    return pl.pallas_call(
        functools.partial(attend_kernel, sz),
        grid=(images,),
        in_specs=[
            per_image(width),
            whole(width, sz.part_one),
            whole(width, sz.part_two),
            whole(8, rows),
            whole(8, rows),
        ],
        out_specs=(
            per_image(3 * width),
            lse_spec,
            per_image(width),
            per_image(width),
            per_image(width),
            whole(8, rows),
            whole(rows, LANES),
            whole(sz.chunk, width),
            whole(sz.chunk, width),
        ),
        out_shape=(
            jax.ShapeDtypeStruct((images, seq, 3 * width), BF),
            jax.ShapeDtypeStruct((images, 16, seq), F32),
            jax.ShapeDtypeStruct((images, seq, width), BF),
            jax.ShapeDtypeStruct((images, seq, width), F32),
            jax.ShapeDtypeStruct((images, seq, width), BF),
            jax.ShapeDtypeStruct((8, rows), F32),
            jax.ShapeDtypeStruct((rows, LANES), F32),
            jax.ShapeDtypeStruct((sz.chunk, width), BF),
            jax.ShapeDtypeStruct((sz.chunk, width), BF),
        ),
        scratch_shapes=[pltpu.VMEM((rows, width), BF), pltpu.VMEM((LANES, width), F32)],
        compiler_params=kernel_params(56),
        cost_estimate=SMALL_COST,
        name="attend",
    )(tok, *packed, routes_row, slots)


def own_copies(per_ring, block, in_own, out_own, w_in, w_out):
    copies = []
    for j in range(per_ring):
        cols = slice(j * block, (j + 1) * block)
        copies.append((j, in_own.at[:, cols], w_in.at[j]))
        copies.append((j, out_own.at[cols, :], w_out.at[j]))
    return copies


def far_copies(ring, per_ring, block, first_step, in_far, out_far, w_in, w_out):
    copies = []
    for r in range(ring - 1):
        for j in range(per_ring):
            step, start = first_step + per_ring * r + j, j * block
            at = 0
            for piece in in_far:
                rows = slice(at, at + piece.shape[1])
                copies.append(
                    (step, piece.at[r, :, start : start + block], w_in.at[step, rows, :])
                )
                at += piece.shape[1]
            at = 0
            for piece in out_far:
                first, last = max(at, start), min(at + piece.shape[1], start + block)
                if first < last:
                    copies.append(
                        (
                            step,
                            piece.at[r, first - at : last - at, :],
                            w_out.at[step, first - start : last - start, :],
                        )
                    )
                at += piece.shape[1]
    return copies


def expert_kernel(sz, ring, per_ring, own, far, extra, in_count, out_count, *refs):
    refs = list(refs)
    take = lambda count: [refs.pop(0) for _ in range(count)]
    x_ref, dy_ref = take(2)
    in_own, out_own = take(2) if own else (None, None)
    in_far, out_far = take(in_count if far else 0), take(out_count if far else 0)
    if not own:
        grad_res, res_before, back_before = take(3)
    take(extra)
    hidden_ref, inner_ref = take(2)
    if own:
        grad_res = take(1)[0]
    if far:
        res_ref, back_ref = take(2)
    res_sum, back_sum = take(2)
    acts, hids = take(2), take(2)
    w_in, w_out, sems = take(3)
    steps = w_in.shape[0]
    half, width, experts = sz.half, sz.width, sz.experts
    step = pl.program_id(0)
    diag = iota((half, LANES), 0) == iota((half, LANES), 1)
    block = w_in.shape[2]
    wanted = own_copies(per_ring, block, in_own, out_own, w_in, w_out) if own else []
    if far:
        first_step = per_ring if own else 0
        wanted += far_copies(ring, per_ring, block, first_step, in_far, out_far, w_in, w_out)
    copies = [
        (at, pltpu.make_async_copy(source, target, sems.at[n]))
        for n, (at, source, target) in enumerate(wanted)
    ]

    @pl.when(step == 0)
    def _():
        for _at, copy in copies:
            copy.start()
        if not own:
            res_sum[...] = res_before[...]
            back_sum[...] = back_before[...]
            return
        for e in range(experts):
            at = e * half
            line = x_ref[at : at + 16, 0 : 3 * LANES].astype(F32)[0:1]
            gate = line[:, 0:LANES] + line[:, LANES : 2 * LANES] + line[:, 2 * LANES :]
            gate = jnp.sum(jnp.where(diag, gate, 0.0), axis=1, keepdims=True)
            grad_res[at : at + half, :] = (gate * dy_ref[e].astype(F32)).astype(BF)
        res_sum[...] = jnp.zeros_like(res_sum)
        back_sum[...] = jnp.zeros_like(back_sum)

    for at in range(steps):

        @pl.when(step == at)
        def _(at=at):
            for when, copy in copies:
                if when == at:
                    copy.wait()

    def work():
        chunk = x_ref.shape[0]
        in_ref, out_ref = w_in.at[step], w_out.at[step]
        tile = 256 if block % 256 == 0 else 128
        count = block // tile
        pieces = [slice(n * tile, (n + 1) * tile) for n in range(count)]
        spans = [slice(at, at + min(256, chunk)) for at in range(0, chunk, 256)]

        def enter(n, rows):
            acts[n % 2][rows, :] = dot_nn(x_ref[rows, :], in_ref[:, pieces[n]])
            hids[n % 2][rows, :] = dot_nt(grad_res[rows, :], out_ref[pieces[n], :])

        def activate(n, rows):
            for at in range(rows.start, rows.stop, 32):
                some = slice(at, at + 32)
                act, grad_hidden = acts[n % 2][some, :], hids[n % 2][some, :]
                bell = jnp.exp2(act * act * (-0.5 * LOG2_E))
                base = 1.0 + (ERFC_P * 2.0**-0.5) * jnp.abs(act)
                t = pl.reciprocal(base, approx=True)
                t = t * (2.0 - base * t)
                poly = 0.5 * ERFC_C[-1]
                for coefficient in ERFC_C[-2::-1]:
                    poly = poly * t + 0.5 * coefficient
                tail = poly * (t * bell)
                share = jnp.where(act >= 0.0, 1.0 - tail, tail)
                hidden_ref[some, pieces[n]] = (act * share).astype(BF)
                slope = share + act * (bell * 0.3989422804014327)
                inner_ref[some, pieces[n]] = (grad_hidden * slope).astype(BF)

        def leave(first, last, rows):
            part = slice(first * tile, last * tile)
            res_sum[rows, :] += dot_nn(hidden_ref[rows, part], out_ref[part, :])
            back_sum[rows, :] += dot_nt(inner_ref[rows, part], in_ref[:, part])

        for rows in spans:
            enter(0, rows)
        for n in range(count):
            for rows in spans:
                if n + 1 < count:
                    enter(n + 1, rows)
                elif n:
                    leave(0, n, rows)
                activate(n, rows)
        for rows in spans:
            leave(count - 1, count, rows)

    work()
    if not far:
        return

    @pl.when(step == steps - 1)
    def _():
        for e in range(experts):
            rows = slice(e * half, (e + 1) * half)
            res = res_sum[rows, :].astype(BF)
            res_ref[e] = res
            gate = jnp.sum(dy_ref[e].astype(F32) * res.astype(F32), axis=1, keepdims=True)
            line = jnp.sum(jnp.where(diag, gate, 0.0), axis=0, keepdims=True)
            pieces = [p.astype(F32) for p in split_three(line)]
            line = jnp.concatenate(pieces + [jnp.zeros((1, width - 3 * LANES), F32)], axis=1)
            back = jnp.where(iota((half, width), 0) == 0, line, back_sum[rows, :])
            back_ref[e] = back.astype(BF)


def hidden_block(hidden):
    return next(b for b in (768, 512, 384, 256, 128) if hidden % b == 0)


def call_experts(sz, c, ring, x, dy, own, far, before=(), res=None):
    width, half, chunk, experts = sz.width, sz.half, sz.chunk, sz.experts
    hidden = (own[0] if own else far[0][0]).shape[-1]
    block = hidden_block(hidden)
    per_ring = hidden // block
    steps = per_ring * ((1 if own else 0) + (ring - 1 if far else 0))
    last = bool(far) or ring == 1
    rows_spec = pl.BlockSpec((experts, half, width), lambda s: (0, 0, 0))
    flat_spec = pl.BlockSpec((chunk, width), lambda s: (0, 0))
    wide_spec = pl.BlockSpec((chunk, block), lambda s: (0, s))
    any_spec = pl.BlockSpec(memory_space=pl.ANY)
    weights = [*own, *(far[0] if far else []), *(far[1] if far else [])]
    tile = 256 if block % 256 == 0 else 128
    flat = lambda kind: jax.ShapeDtypeStruct((chunk, width), kind)
    rows = jax.ShapeDtypeStruct((experts, half, width), BF)
    both = jax.ShapeDtypeStruct((experts, 2 * half, width), BF)
    chunk_spec = pl.BlockSpec((experts, half, width), lambda s: (0, c, 0))
    wide = jax.ShapeDtypeStruct((chunk, steps * block), BF)
    out_specs, out_shape = [wide_spec, wide_spec], [wide, wide]
    if own:
        out_specs, out_shape = out_specs + [flat_spec], out_shape + [flat(BF)]
    sums = [pltpu.VMEM((chunk, width), F32)] * 2
    if last:
        out_specs, out_shape = out_specs + [chunk_spec, rows_spec], out_shape + [both, rows]
    else:
        out_specs, out_shape, sums = out_specs + [flat_spec] * 2, out_shape + [flat(F32)] * 2, []
    counts = (len(far[0]), len(far[1])) if far else (0, 0)
    given = [] if res is None else [res]
    return pl.pallas_call(
        functools.partial(
            expert_kernel, sz, ring, per_ring, bool(own), last, len(given), *counts
        ),
        grid=(steps,),
        in_specs=[flat_spec, pl.BlockSpec((experts, half, width), lambda s: (0, c, 0))]
        + [any_spec] * len(weights)
        + [flat_spec] * len(before)
        + [any_spec] * len(given),
        input_output_aliases={2 + len(weights) + len(before): 3} if given else {},
        out_specs=out_specs,
        out_shape=out_shape,
        scratch_shapes=sums
        + [pltpu.VMEM((chunk, tile), F32)] * 4
        + [
            pltpu.VMEM((steps, width, block), BF),
            pltpu.VMEM((steps, block, width), BF),
            pltpu.SemaphoreType.DMA((steps * (2 + sum(counts)),)),
        ],
        compiler_params=kernel_params(56),
        cost_estimate=SMALL_COST,
        name="experts",
    )(x, dy, *weights, *before, *given)


def weight_grad_kernel(
    x_one, x_two, grad_one, grad_two, hid_one, hid_two, inn_one, inn_two, _early, *refs
):
    x_t, grad_t = refs[-2:]
    count = (len(refs) - 2) // 2
    gi_refs, go_refs = refs[:count], refs[count : 2 * count]
    chunk = x_one.shape[0]

    @pl.when(pl.program_id(0) == 0)
    def _():
        x_t[:, :chunk] = x_one[...].T
        x_t[:, chunk:] = x_two[...].T
        grad_t[:, :chunk] = grad_one[...].T
        grad_t[:, chunk:] = grad_two[...].T

    grad_in = dot_nn(x_t[:, :chunk], inn_one[...]) + dot_nn(x_t[:, chunk:], inn_two[...])
    at = 0
    for ref in gi_refs:
        ref[...] = grad_in[at : at + ref.shape[0]].astype(ref.dtype)
        at += ref.shape[0]
    grad_out = dot_nn(grad_t[:, :chunk], hid_one[...]) + dot_nn(grad_t[:, chunk:], hid_two[...])
    grad_out = grad_out.T
    at = 0
    for ref in go_refs:
        ref[...] = grad_out[:, at : at + ref.shape[1]].astype(ref.dtype)
        at += ref.shape[1]


def call_weight_grads(sz, ring, hidden, far, flats, wides, early):
    width, chunk = sz.width, sz.chunk
    block = next(b for b in (512, 384, 256, 128) if hidden % b == 0)
    per_ring = hidden // block
    count = (ring - 1) * per_ring if far else per_ring
    flat_spec = pl.BlockSpec((chunk, width), lambda s: (0, 0))
    wide_spec = lambda first: pl.BlockSpec((chunk, block), lambda s: (0, first + s))
    wide_specs = [wide_spec(per_ring if far and whole else 0) for _array, whole in wides]
    if far:
        in_cuts = out_cuts = (width // 3, width - width // 3)
        out_specs = [
            pl.BlockSpec((None, part, block), lambda s: (s // per_ring, 0, s % per_ring))
            for part in in_cuts
        ] + [
            pl.BlockSpec((None, block, part), lambda s: (s // per_ring, s % per_ring, 0))
            for part in out_cuts
        ]
        out_shape = [jax.ShapeDtypeStruct((ring - 1, part, hidden), BF) for part in in_cuts] + [
            jax.ShapeDtypeStruct((ring - 1, hidden, part), BF) for part in out_cuts
        ]
    else:
        out_specs = (
            pl.BlockSpec((width, block), lambda s: (0, s)),
            pl.BlockSpec((block, width), lambda s: (s, 0)),
        )
        out_shape = (
            jax.ShapeDtypeStruct((width, hidden), BF),
            jax.ShapeDtypeStruct((hidden, width), BF),
        )
    return pl.pallas_call(
        weight_grad_kernel,
        grid=(count,),
        in_specs=[flat_spec] * 4 + wide_specs + [pl.BlockSpec(memory_space=pl.ANY)],
        out_specs=out_specs,
        out_shape=out_shape,
        scratch_shapes=[pltpu.VMEM((width, 2 * chunk), BF), pltpu.VMEM((width, 2 * chunk), BF)],
        compiler_params=kernel_params(56),
        cost_estimate=pl.CostEstimate(
            flops=8 * chunk * width * block * count,
            bytes_accessed=8 * chunk * block * count + 8 * width * block * count,
            transcendentals=0,
        ),
        name="weight_grads",
    )(*flats, *(array for array, _whole in wides), early)


def combine_kernel(
    sz,
    back_one_ref,
    back_two_ref,
    slot_ref,
    slot_col_ref,
    gate_ref,
    routes_ref,
    proj_ref,
    tail_ref,
    dy_ref,
    after_ref,
    normed_ref,
    mixed_ref,
    _early,
    grad_after_ref,
    grad_mixed_ref,
    proj_grad_ref,
    small_ref,
    tail_t,
    from_router,
    branch_all,
):
    width, seq, rows, half, chunk = sz.width, sz.seq_pad, sz.rows, sz.half, sz.chunk
    step = pl.program_id(0)
    first = sz.experts

    @pl.when(step == 0)
    def _():
        tail_t[...] = tail_ref[...].astype(F32).T
        group = max(1, LANES // half)
        metas = []
        for ref in (back_one_ref, back_two_ref):
            for e0 in range(0, sz.experts, group):
                line = jnp.zeros((1, 3 * LANES), F32)
                for g in range(group):
                    at = (e0 + g) * half
                    one = ref[at : at + 16, 0 : 3 * LANES].astype(F32)
                    pieces = [one[:, m * LANES : (m + 1) * LANES] for m in range(3)]
                    if g:
                        pieces = [pltpu.roll(p, g * half, axis=1) for p in pieces]
                    line += jnp.concatenate([p[0:1] for p in pieces], axis=1)
                metas.append(line)
        part = iota((16, 2 * chunk), 0)
        coded = jnp.zeros((16, 2 * chunk), F32)
        for m in range(3):
            line = jnp.concatenate([x[:, m * LANES : (m + 1) * LANES] for x in metas], axis=1)
            coded = jnp.where(part == m, line, coded)
        coded = coded.astype(BF)
        grads = []
        for k in range(sz.choose):
            ids = iota((256, rows), 0)
            total = jnp.zeros((16, rows), F32)
            for start in range(0, 2 * chunk, 256):
                pick = ones_where(ids + start == slot_ref[k : k + 1]).astype(BF)
                total += dot_nn(coded[:, start : start + 256], pick)
            grads.append(jnp.sum(total, axis=0, keepdims=True))
        gates = [gate_ref[k : k + 1] for k in range(sz.choose)]
        mean_grad = functools.reduce(jnp.add, [g * v for g, v in zip(gates, grads)])
        kinds = iota((LANES, rows), 0)
        logits_grad = jnp.zeros((LANES, rows), F32)
        for k in range(sz.choose):
            chosen = gates[k] * (grads[k] - mean_grad)
            logits_grad = jnp.where(kinds == routes_ref[k : k + 1], chosen, logits_grad)
        logits_grad = logits_grad.astype(BF)
        small_ref[...] = dot_nn(logits_grad, normed_ref[...].reshape(rows, width))
        from_router[...] = dot_tn(logits_grad, tail_t[...].astype(BF))

    here = pl.ds(step * seq, seq)
    slot_col = slot_col_ref[here, :]
    upstream = from_router[here, :]
    for c, ref in enumerate((back_one_ref, back_two_ref)):
        ids = iota((seq, chunk), 1) + c * chunk
        pick = ids == slot_col[:, 0:1]
        for k in range(1, sz.choose):
            pick = pick | (ids == slot_col[:, k : k + 1])
        upstream += dot_nn(ones_where(pick).astype(BF), ref[...])
    normal, inv = norm_parts(after_ref[...])
    grad_after = dy_ref[...].astype(F32) + norm_back(
        upstream, tail_t[first + 2 : first + 3], normal, inv
    )
    live = iota((seq, 1), 0) < SEQ
    grad_after = jnp.where(live, grad_after, 0.0)
    upstream = jnp.where(live, upstream, 0.0)
    grad_after_ref[...] = grad_after
    branch = grad_after.astype(BF)
    branch_all[here, :] = branch
    grad_mixed_ref[...] = dot_nn(branch, proj_ref[...]).astype(BF)
    small_ref[first + 2 : first + 3, :] += jnp.sum(upstream * normal, axis=0, keepdims=True)
    small_ref[first + 3 : first + 4, :] += jnp.sum(upstream, axis=0, keepdims=True)

    @pl.when(step == sz.images - 1)
    def _():
        proj_grad_ref[...] = dot_tn(
            branch_all[...], mixed_ref[...].reshape(rows, width)
        ).astype(BF)


def call_combine(
    sz,
    back_one,
    back_two,
    slots,
    slot_col,
    gates,
    routes_row,
    packed,
    dy,
    attended,
    normed,
    mixed,
    early,
):
    images, seq, width, rows = sz.images, sz.seq_pad, sz.width, sz.rows
    per_image = lambda size: pl.BlockSpec((None, seq, size), lambda i: (i, 0, 0))
    whole = lambda *shape: pl.BlockSpec(shape, lambda i: (0,) * len(shape))
    return pl.pallas_call(
        functools.partial(combine_kernel, sz),
        grid=(images,),
        in_specs=[
            whole(sz.chunk, width),
            whole(sz.chunk, width),
            whole(8, rows),
            whole(rows, LANES),
            whole(8, rows),
            whole(8, rows),
            pl.BlockSpec((width, width), lambda i: (0, 1)),
            pl.BlockSpec((width, LANES), lambda i: (0, 2 * width // LANES)),
            per_image(width),
            per_image(width),
            whole(images, seq, width),
            whole(images, seq, width),
            pl.BlockSpec(memory_space=pl.ANY),
        ],
        out_specs=(
            per_image(width),
            per_image(width),
            whole(width, width),
            whole(LANES, width),
        ),
        out_shape=(
            jax.ShapeDtypeStruct((images, seq, width), F32),
            jax.ShapeDtypeStruct((images, seq, width), BF),
            jax.ShapeDtypeStruct((width, width), BF),
            jax.ShapeDtypeStruct((LANES, width), F32),
        ),
        scratch_shapes=[
            pltpu.VMEM((LANES, width), F32),
            pltpu.VMEM((rows, width), F32),
            pltpu.VMEM((rows, width), BF),
        ],
        compiler_params=kernel_params(56),
        cost_estimate=pl.CostEstimate(
            flops=4 * rows * width * width + 4 * rows * sz.chunk * width,
            bytes_accessed=rows * width * 16 + 4 * sz.chunk * width + 4 * width * width,
            transcendentals=0,
        ),
        name="combine",
    )(
        back_one,
        back_two,
        slots,
        slot_col,
        gates,
        routes_row,
        packed[1],
        packed[1],
        dy,
        attended,
        normed,
        mixed,
        early,
    )


def attend_back_kernel(
    sz,
    tok_ref,
    w_one_ref,
    w_two_ref,
    qkv_ref,
    lse_ref,
    grad_mixed_ref,
    grad_after_ref,
    proj_grad_ref,
    small_ref,
    core_ref,
    _early,
    tok_grad_ref,
    *refs,
):
    packed_refs = refs[:-4]
    tail_t, normed_all, grad_all, small_sum = refs[-4:]
    width, seq, rows = sz.width, sz.seq_pad, sz.rows
    step = pl.program_id(0)
    first = sz.experts

    @pl.when(step == 0)
    def _():
        tail_t[...] = w_two_ref[:, 2 * width :].astype(F32).T
        small_sum[...] = small_ref[...]

    here = pl.ds(step * seq, seq)
    gain, bias = tail_t[first : first + 1], tail_t[first + 1 : first + 2]
    normal, inv = norm_parts(tok_ref[...].astype(F32))
    normed_all[here, :] = (normal * gain + bias).astype(BF)
    key_ok = iota((seq, seq), 0) < SEQ
    pair_lane = iota((1, LANES), 1) // HEAD
    for j in range(HEADS // 2):
        at = j * LANES
        q = qkv_ref[:, at : at + LANES]
        key = qkv_ref[:, width + at : width + at + LANES]
        val = qkv_ref[:, 2 * width + at : 2 * width + at + LANES]
        grad = grad_mixed_ref[:, at : at + LANES]
        sum_q = jnp.zeros((seq, LANES), F32)
        sum_k = jnp.zeros((seq, LANES), F32)
        sum_v = jnp.zeros((seq, LANES), F32)
        for a in range(2):
            own = ones_where(pair_lane == a).astype(BF)
            scaled = own * HEAD**-0.5
            q_own, grad_own = q * scaled, grad * own
            scores = dot_nt(key, q_own)
            lse = lse_ref[2 * j + a : 2 * j + a + 1, :]
            probs = jnp.where(key_ok, jnp.exp(scores - lse), 0.0)
            grad_probs = dot_nt(val, grad_own)
            sum_v += dot_nn(probs.astype(BF), grad_own)
            delta = jnp.sum(grad_probs * probs, axis=0, keepdims=True)
            grad_scores = (probs * (grad_probs - delta)).astype(BF)
            sum_q += dot_tn(grad_scores, key * scaled)
            sum_k += dot_nn(grad_scores, q_own)
        grad_all[here, at : at + LANES] = sum_q.astype(BF)
        grad_all[here, width + at : width + at + LANES] = sum_k.astype(BF)
        grad_all[here, 2 * width + at : 2 * width + at + LANES] = sum_v.astype(BF)
    upstream = dot_nt(grad_all[here, : 2 * width], w_one_ref[...])
    upstream += dot_nt(grad_all[here, 2 * width :], w_two_ref[:, :width])
    tok_grad_ref[...] = grad_after_ref[...] + norm_back(upstream, gain, normal, inv)
    small_sum[first : first + 1, :] += jnp.sum(upstream * normal, axis=0, keepdims=True)
    small_sum[first + 1 : first + 2, :] += jnp.sum(upstream, axis=0, keepdims=True)

    @pl.when(step == sz.images - 1)
    def _():
        parts = (
            dot_tn(normed_all[...], grad_all[...]),
            proj_grad_ref[...].astype(F32),
            small_sum[...].T,
        )
        if len(packed_refs) == 1:
            at = 0
            for part in parts:
                size = part.shape[1]
                packed_refs[0][:, at : at + size] = part.astype(BF)
                at += size
            return
        keep_one, send_one, keep_two, send_two = packed_refs
        n_dp, ring, shard, _ = keep_one.shape
        first_core = core_ref[0] == 0

        def put(keep, send, at, part, part_lanes):
            size = part_lanes.stop - part_lanes.start
            for d in range(n_dp):
                for r in range(ring):
                    row = (d * ring + r) * 2 * shard
                    zero = part[row : row + shard, part_lanes]
                    one = part[row + shard : row + 2 * shard, part_lanes]
                    place = (d, r) if keep is keep_one else (r, d)
                    keep[(*place, slice(None), slice(at, at + size))] = jnp.where(
                        first_core, zero, one
                    ).astype(BF)
                    send[(*place, slice(None), slice(at, at + size))] = jnp.where(
                        first_core, one, zero
                    ).astype(BF)

        put(keep_one, send_one, 0, parts[0], slice(0, 2 * width))
        put(keep_two, send_two, 0, parts[0], slice(2 * width, 3 * width))
        put(keep_two, send_two, width, parts[1], slice(0, width))
        put(keep_two, send_two, 2 * width, parts[2], slice(0, parts[2].shape[1]))


def call_attend_back(
    sz, tok, packed, qkv, lse, grad_mixed, grad_after, proj_grad, small, core, early, out_dims
):
    images, seq, width, rows = sz.images, sz.seq_pad, sz.width, sz.rows
    per_image = lambda size: pl.BlockSpec((None, seq, size), lambda i: (i, 0, 0))
    lse_spec = pl.BlockSpec((None, 16, seq), lambda i: (i, 0, 0))
    whole = lambda *shape: pl.BlockSpec(shape, lambda i: (0,) * len(shape))
    return pl.pallas_call(
        functools.partial(attend_back_kernel, sz),
        grid=(images,),
        in_specs=[
            per_image(width),
            whole(width, sz.part_one),
            whole(width, sz.part_two),
            per_image(3 * width),
            lse_spec,
            per_image(width),
            per_image(width),
            whole(width, width),
            whole(LANES, width),
            pl.BlockSpec(memory_space=pltpu.SMEM),
            pl.BlockSpec(memory_space=pl.ANY),
        ],
        out_specs=(per_image(width), *(whole(*dims) for dims in out_dims)),
        out_shape=(
            jax.ShapeDtypeStruct((images, seq, width), F32),
            *(jax.ShapeDtypeStruct(dims, BF) for dims in out_dims),
        ),
        scratch_shapes=[
            pltpu.VMEM((LANES, width), F32),
            pltpu.VMEM((rows, width), BF),
            pltpu.VMEM((rows, 3 * width), BF),
            pltpu.VMEM((LANES, width), F32),
        ],
        compiler_params=kernel_params(56),
        cost_estimate=pl.CostEstimate(
            flops=12 * rows * width * width + 10 * rows * seq * width,
            bytes_accessed=4 * width * sz.packed + rows * width * 18,
            transcendentals=rows * seq * HEADS,
        ),
        name="attend_back",
    )(tok, *packed, qkv, lse, grad_mixed, grad_after, proj_grad, small, core, early)


def output_kernel(sz, res_ref, slot_col_ref, gate_col_ref, after_ref, out_ref):
    seq, chunk = sz.seq_pad, sz.chunk
    here = pl.ds(pl.program_id(0) * seq, seq)
    slot_col = slot_col_ref[here, :]
    gate_col = gate_col_ref[here, :]
    moe = jnp.zeros((seq, sz.width), F32)
    for k in range(sz.choose):
        rows = jnp.zeros((seq, sz.width), F32)
        for c in range(2):
            ids = iota((seq, chunk), 1) + c * chunk
            res = res_ref[:, c * sz.half : (c + 1) * sz.half, :].reshape(chunk, sz.width)
            rows += dot_nn(ones_where(ids == slot_col[:, k : k + 1]).astype(BF), res)
        moe += gate_col[:, k : k + 1] * rows
    out_ref[...] = (after_ref[...] + moe).astype(BF)


def call_output(sz, res, slot_col, gate_col, after):
    images, seq, width, rows = sz.images, sz.seq_pad, sz.width, sz.rows
    per_image = pl.BlockSpec((None, seq, width), lambda i: (i, 0, 0))
    whole = lambda *shape: pl.BlockSpec(shape, lambda i: (0,) * len(shape))
    return pl.pallas_call(
        functools.partial(output_kernel, sz),
        grid=(images,),
        in_specs=[
            whole(sz.experts, 2 * sz.half, width),
            whole(rows, LANES),
            whole(rows, LANES),
            per_image,
        ],
        out_specs=per_image,
        out_shape=jax.ShapeDtypeStruct((images, seq, width), BF),
        compiler_params=kernel_params(24),
        cost_estimate=SMALL_COST,
        name="output",
    )(res, slot_col, gate_col, after)


def adam_update(weight, gradient, moment_one, moment_two, clip_scale, rate_val, decay_val):
    clipped = gradient * clip_scale
    first_new = BETA_ONE * moment_one + (1.0 - BETA_ONE) * clipped
    second_new = BETA_TWO * moment_two + (1.0 - BETA_TWO) * clipped * clipped
    first_hat = first_new / (1.0 - BETA_ONE**STEP)
    second_hat = second_new / (1.0 - BETA_TWO**STEP)
    return (
        first_new,
        second_new,
        weight - rate_val * (first_hat / (jnp.sqrt(second_hat) + ADAM_EPS) + decay_val * weight),
    )


def exchange(array):
    return lax.all_to_all(array, GROUP, split_axis=0, concat_axis=0, tiled=True)


class Gather:
    def __init__(self, array):
        self.rank, self.done, self.array = {}, [], array
        for axis in ALL:
            for bit in reversed(range(lax.axis_size(axis).bit_length() - 1)):
                self.rank[axis, bit] = len(self.rank)

    def bits(self, axis):
        return [key for key in self.rank if key[0] == axis]

    def advance(self, keys):
        for key in keys:
            self.double(*key)
        return self.array

    def part(self, lanes):
        other = Gather(self.array[..., lanes])
        other.done = list(self.done)
        return other

    def double(self, axis, bit):
        array, flip = self.array, 1 << bit
        other = lax.ppermute(array, axis, [(s, s ^ flip) for s in range(lax.axis_size(axis))])
        at = sum(self.rank[key] < self.rank[axis, bit] for key in self.done)
        here = (lax.axis_index(axis) >> bit) & 1
        side = lax.broadcasted_iota(jnp.int32, (1,) * at + (2,) + (1,) * (array.ndim - at), at)
        self.array = jnp.where(side == here, jnp.expand_dims(array, at), jnp.expand_dims(other, at))
        self.done.append((axis, bit))

    def wait(self, *others):
        self.array = after(self.array, *others)


def scatter_ring(grads, axis):
    count, here = lax.axis_size(axis), lax.axis_index(axis)
    pick = lambda at: lax.dynamic_index_in_dim(grads, at % count, 0, keepdims=False)
    total = pick(here).astype(F32)
    for r in range(1, count):
        ahead = [(s, (s + r) % count) for s in range(count)]
        total += lax.ppermute(pick(here + r), axis, ahead).astype(F32)
    return total


def after(array, *others):
    return lax.optimization_barrier((array, *others))[0]


def on_device(
    tokens,
    out_grad,
    routes,
    slot_order,
    norm_params,
    qkv_weight,
    proj_weight,
    router_weight,
    inner_weight,
    outer_weight,
    norm_moment,
    norm_second,
    qkv_moment,
    qkv_second,
    proj_moment,
    proj_second,
    router_moment,
    router_second,
    inner_moment,
    inner_second,
    outer_moment,
    outer_second,
):
    tok_count, width = tokens.shape
    choose = routes.shape[1]
    experts = router_weight.shape[1]
    sz = Sizes(tok_count, width, choose, experts)
    images, seq, rows = sz.images, sz.seq_pad, sz.rows
    ring = lax.axis_size("row")
    n_dp, n_col = lax.axis_size("dp"), lax.axis_size("col")
    shard = qkv_weight.shape[0]

    gather = Gather(
        jnp.concatenate(
            [
                qkv_weight.astype(BF).reshape(shard, 3 * width),
                proj_weight.astype(BF),
                router_weight.astype(BF),
                norm_params.astype(BF),
                jnp.zeros((shard, sz.packed - 4 * width - experts - 4), BF),
            ],
            axis=1,
        )
    )
    in_own = lax.optimization_barrier(inner_weight[0].astype(BF))
    out_own = lax.optimization_barrier(outer_weight[0].astype(BF))

    def from_ahead(array, r):
        return lax.ppermute(array, "row", [(s, (s - r) % ring) for s in range(ring)])

    def to_ahead(array, r):
        return lax.ppermute(array, "row", [(s, (s + r) % ring) for s in range(ring)])

    def from_row(array):
        if ring == 1:
            return array[None]
        return jnp.stack([from_ahead(array, r) for r in range(1, ring)])

    cut = width // 4
    in_top = [from_row(in_own[:cut]), from_row(in_own[cut : 2 * cut])]

    def pad_rows(array):
        array = array.reshape(images, SEQ, array.shape[1])
        return jnp.pad(array, ((0, 0), (0, seq - SEQ), (0, 0)))

    tok_pad, dy_pad = pad_rows(tokens), pad_rows(out_grad)
    order = slot_order[0]
    order = (order % choose) * rows + order // choose
    order = jnp.pad(order, (0, sz.rank - sz.pairs), constant_values=-1).reshape(1, sz.rank)
    fill = ((0, 0), (0, rows - tok_count))
    routes_flat = jnp.pad(routes.T, fill, constant_values=-1).reshape(1, choose * rows)
    dy_flat = jnp.pad(out_grad, ((0, rows - tok_count), (0, 0)))
    flat_slots, dy_send = call_slots(sz, order, routes_flat, dy_flat)
    slots = jnp.pad(
        flat_slots[:, :tok_count].reshape(8, images, SEQ),
        ((0, 0), (0, 0), (0, seq - SEQ)),
        constant_values=-1,
    ).reshape(8, rows)
    slot_col = jnp.pad(slots.T, ((0, 0), (0, LANES - 8)))
    routes_row = jnp.pad(
        slots[choose : 2 * choose], ((0, 8 - choose), (0, 0)), constant_values=-1
    )
    dp_bits, row_bits, col_bits = gather.bits("dp"), gather.bits("row"), gather.bits("col")
    gather.advance(dp_bits[:-1])
    gather.wait(flat_slots, in_top[0])
    part_one = gather.part(slice(0, sz.part_one))
    part_two = gather.part(slice(sz.part_one, sz.packed))
    part_one.advance(dp_bits[-1:])
    part_two.advance(dp_bits[-1:])
    dy_there = exchange(after(dy_send, part_one.array, part_two.array, in_top[1]))
    one_row = part_one.advance(row_bits)
    part_one.wait(tok_pad, out_own)
    part_one = part_one.advance(col_bits)
    part_two = part_two.advance(row_bits + col_bits)
    packed = (part_one.reshape(width, sz.part_one), part_two.reshape(width, sz.part_two))
    in_far = [*in_top, from_row(after(in_own[2 * cut :], one_row))]
    cut = out_own.shape[0] * 9 // 32 // 16 * 16
    out_far = [from_row(after(out_own[:cut], one_row)), from_row(out_own[cut:])]

    qkv, lse, mixed, attended, normed, gates, gate_col, send_one, send_two = call_attend(
        sz, tok_pad, packed, routes_row, slots
    )

    def exchange_rows(array):
        return exchange(array.reshape(experts, sz.half, width)).reshape(sz.chunk, width)

    x_one = exchange_rows(after(send_one, dy_there, in_far[2], out_far[0]))
    x_two = exchange_rows(after(send_two, x_one, out_far[1], dy_pad, slot_col))
    own, far = [in_own, out_own], [in_far, out_far] if ring > 1 else None
    hidden_one, inner_one, grad_one, res_one, back_one = call_experts(
        sz, 0, ring, x_one, dy_there, own, far
    )
    hidden_two, inner_two, grad_two, res_both, back_two = call_experts(
        sz, 1, ring, x_two, dy_there, own, far, res=res_one
    )
    wides = [(array, True) for array in (hidden_one, hidden_two, inner_one, inner_two)]
    flats = (x_one, x_two, grad_one, grad_two)
    first_back = back_two
    back_one = exchange(back_one).reshape(sz.chunk, width)
    back_two = exchange(back_two).reshape(sz.chunk, width)
    hidden = in_own.shape[1]
    away = None
    if ring > 1:
        away = call_weight_grads(sz, ring, hidden, True, flats, wides, first_back)
    in_grad, out_grad_own = call_weight_grads(
        sz, ring, hidden, False, flats, wides, first_back if away is None else away[0]
    )
    kept_grads = (in_grad, out_grad_own)
    in_sent, out_sent = [[], []], [[], []]
    if ring > 1:
        send = lambda array: [to_ahead(part, r + 1) for r, part in enumerate(array)]
        in_sent, out_sent = [send(away[0]), send(away[1])], [send(away[2]), send(away[3])]
        for top, low in zip(*in_sent):
            in_grad = in_grad.astype(F32) + jnp.concatenate([top, low]).astype(F32)
        for top, low in zip(*out_sent):
            out_grad_own = out_grad_own.astype(F32) + jnp.concatenate([top, low], axis=1).astype(F32)
    res = exchange(after(res_both, *kept_grads, *in_sent[0]))

    grad_after, grad_mixed, proj_grad, small = call_combine(
        sz,
        back_one,
        back_two,
        slots,
        slot_col,
        gates,
        routes_row,
        packed,
        dy_pad,
        attended,
        normed,
        mixed,
        kept_grads[0],
    )
    direct = shard % 8 == 0 and n_col == 2
    one_dims = (n_dp, ring, shard, sz.part_one)
    two_dims = (ring, n_dp, shard, sz.part_two)
    core = lax.axis_index("col")
    tok_grad, *packed_grads = call_attend_back(
        sz,
        tok_pad,
        packed,
        qkv,
        lse,
        grad_mixed,
        grad_after,
        proj_grad,
        small,
        core.astype(jnp.int32).reshape(1),
        kept_grads[0],
        [one_dims, one_dims, two_dims, two_dims] if direct else [(width, sz.packed)],
    )
    block_out = call_output(sz, res, slot_col, gate_col, attended)

    if direct:
        keep_one, send_one, keep_two, send_two = packed_grads
        swap = lambda sent: lax.ppermute(sent, "col", [(0, 1), (1, 0)]).astype(F32)
        sum_one = keep_one.astype(F32) + swap(after(send_one, *in_sent[1], *out_sent[0]))
        sum_two = keep_two.astype(F32) + swap(after(send_two, *in_sent[1], *out_sent[0]))
    else:
        grads = packed_grads[0].reshape(n_dp, ring, n_col, shard, sz.packed)
        grads = scatter_ring(grads.transpose(2, 0, 1, 3, 4), "col")
        sum_one = grads[..., : sz.part_one]
        sum_two = grads[..., sz.part_one :].transpose(1, 0, 2, 3)

    def scatter_dp(grads):
        return lax.all_to_all(grads.astype(BF), "dp", split_axis=0, concat_axis=0, tiled=True)

    sum_one = jnp.sum(scatter_dp(after(sum_one, res)).astype(F32), axis=0)
    sum_two = scatter_ring(after(sum_two.astype(BF), *out_sent[1], block_out), "row")
    block_out = block_out[:, :SEQ].reshape(tok_count, width)
    tok_grad = tok_grad[:, :SEQ].reshape(tok_count, width)
    parts = scatter_dp(after(sum_two, sum_one, block_out, tok_grad))
    share_one = scatter_ring(sum_one.astype(BF), "row")
    share_two = jnp.sum(parts.astype(F32), axis=0)
    share = jnp.concatenate([share_one, share_two], axis=1)
    qkv_share = share[:, : 3 * width].reshape(shard, 3, width)
    proj_share = share[:, 3 * width : 4 * width]
    router_share = share[:, 4 * width : 4 * width + experts]
    norm_share = share[:, 4 * width + experts : 4 * width + experts + 4]

    in_grad, out_grad_own = in_grad.astype(F32), out_grad_own.astype(F32)
    local_square = (
        jnp.sum(share * share) + jnp.sum(in_grad * in_grad) + jnp.sum(out_grad_own * out_grad_own)
    )
    count = n_dp * ring * n_col
    squares = lax.all_to_all(
        jnp.broadcast_to(local_square, (count, 1, LANES)), ALL, split_axis=0, concat_axis=0, tiled=True
    )
    square_sum = jnp.sum(squares[:, 0, 0])
    grad_norm = jnp.sqrt(square_sum)
    clip_scale = jnp.minimum(1.0, CLIP_NORM / (grad_norm + 1e-06))
    outs = [
        block_out,
        tok_grad,
        grad_norm,
    ]
    outs += adam_update(
        norm_params, norm_share, norm_moment, norm_second, clip_scale, RATE_NORM, 0.0
    )
    for weight, grad, moment, second in (
        (qkv_weight, qkv_share, qkv_moment, qkv_second),
        (proj_weight, proj_share, proj_moment, proj_second),
        (router_weight, router_share, router_moment, router_second),
        (inner_weight, in_grad[None], inner_moment, inner_second),
        (outer_weight, out_grad_own[None], outer_moment, outer_second),
    ):
        outs += adam_update(weight, grad, moment, second, clip_scale, RATE_MATRIX, DECAY_MATRIX)
    return tuple(outs)


def solution(mesh):
    rows = P(ALL, None)
    cube = P(ALL, None, None)
    inner = P(GROUP, None, "row")
    outer = P(GROUP, "row", None)
    return jax.shard_map(
        on_device,
        mesh=mesh,
        in_specs=(rows,) * 5
        + (cube, rows, rows, inner, outer)
        + (rows, rows, cube, cube, rows, rows, rows, rows, inner, inner, outer, outer),
        out_specs=(rows, rows, P())
        + (rows,) * 3
        + (cube,) * 3
        + (rows,) * 6
        + (inner,) * 3
        + (outer,) * 3,
        check_vma=False,
    )
```
